768 devices in a mesh: samp: 24 (over x, z_lo), space: 32 (over z_hi, y, core).
Axes of the slice: x: 4, y: 8, z: 12 (z_hi: 2, z_lo: 6; z = z_hi * 6 + z_lo), core: 2. Of those that a mesh axis runs over, the one named last changes fastest.
Arguments:
- tide_state: float32 [8, 2, 1024, 3072], P(None, None, 'space', 'samp'), may hold values from -6 to 6
- forcing: float32 [8, 2, 1024, 3072], P(None, None, 'space', 'samp'), may hold values from -6 to 6
- wet_mask: int32 [1024, 3072], P('space', 'samp'), may hold values 0 or 1
- depth_band: int32 [1024, 3072], P('space', 'samp'), may hold values from 0 to 7
- drag_table: float32 [8], replicated, may hold values from 0.02 to 0.2
- stiff_table: float32 [8], replicated, may hold values from 0.25 to 2
- sample_times: float32 [48], replicated, may hold values from 0 to 720
- zonal_inverse: float32 [8, 128, 128], replicated, may hold values from -0.5 to 1.5
- meridional_inverse: float32 [8, 512, 512], replicated, may hold values from -0.5 to 1.5
Outputs:
- new_state: float32 [8, 2, 1024, 3072], P(None, None, 'space', 'samp')
The draws below stay inside these ranges and needn't reach their ends.
All inputs are finite; a program needn't handle non-finite values. No bound on the sum of `wet_mask` on one device may be relied on, other than what follows from the above.
Results may differ from the reference program's by a relative error of at most 0.00013.
Values sent between devices are 32-bit elements; how exact they have to be, the bound alone decides.
A program may use at most 64 MiB of HBM per device.

```python
import math
import jax
import jax.numpy as jnp
from jax import lax

K = 8
SAMPLES = 48
NB = 8
LB = 128
LM = 512
ITERS = 2
NY = 1024
NX = 3072


def inverse_blocks(key, width):
    diag_key, noise_key = jax.random.split(key)
    diagonal = jax.random.uniform(diag_key, (K, width), jnp.float32, 0.6, 1.3)
    spread = jnp.clip(jax.random.normal(noise_key, (K, width, width), jnp.float32), -3.0, 3.0)
    spread = spread * (0.5 / width ** 0.5)
    return spread + diagonal[:, :, None] * jnp.eye(width, dtype=jnp.float32)[None]


def draw_zonal_inverse(key, part):
    return inverse_blocks(jax.random.fold_in(key, 11), LB)


def draw_meridional_inverse(key, part):
    return inverse_blocks(jax.random.fold_in(key, 23), LM)


def set_ends(values, own_key, least, high):
    place = [jax.random.randint(jax.random.fold_in(own_key, axis), (), 0, length) for axis, length in enumerate(values.shape)]
    widest = values.shape.index(max(values.shape))
    neighbour = place[:widest] + [(place[widest] + 1) % values.shape[widest]] + place[widest + 1:]
    return values.at[tuple(place)].set(least).at[tuple(neighbour)].set(high)


def block_levels(own_key, dims, cuts, smallest, top_value):
    factor_of, own = 1.0, jax.random.fold_in(own_key, 6)
    for position, blocks in cuts:
        heights = jnp.exp(jax.random.uniform(jax.random.fold_in(own, position), (blocks,), jnp.float32, smallest / len(cuts), top_value / len(cuts)))
        factor_of = factor_of * jnp.repeat(heights, dims[position] // blocks).reshape([-1 if axis == position else 1 for axis in range(len(dims))])
    return factor_of


def normal_values(rng, dims, scale, limit, cuts=(), kind=jnp.bfloat16):
    values = scale * jax.random.normal(rng, dims, jnp.float32)
    if cuts:
        values = values * block_levels(rng, dims, cuts, -0.22, 0.18)
    return jnp.clip(values, -limit, limit).astype(kind)


def setup_inputs(seed: int = 0) -> dict:
    key_list = jax.random.split(jax.random.key(seed), 10)
    tide_state = normal_values(key_list[0], (K, 2, NY, NX), 1.0, 6.0, ((2, 32), (3, 24)), jnp.float32)
    forcing = normal_values(key_list[1], (K, 2, NY, NX), 1.0, 6.0, ((2, 32), (3, 24)), jnp.float32)
    wet_mask = set_ends((jax.random.randint(key_list[2], (NY, NX), 0, 5) < 4).astype(jnp.int32), jax.random.fold_in(key_list[2], 1), 0, 1)
    depth_band = set_ends(jax.random.randint(key_list[3], (NY, NX), 0, NB), jax.random.fold_in(key_list[3], 1), 0, NB - 1).astype(jnp.int32)
    drag_table = jnp.clip(jnp.exp(jax.random.uniform(key_list[4], (NB,), jnp.float32, math.log(0.02), math.log(0.2))), 0.02, 0.2)
    stiff_table = jnp.clip(jnp.exp(jax.random.uniform(key_list[5], (NB,), jnp.float32, math.log(0.25), math.log(2.0))), 0.25, 2.0)
    sample_times = jnp.clip(jax.random.uniform(key_list[6], (SAMPLES,), jnp.float32, 0.0, 720.0), 0.0, 720.0)
    zonal_inverse = draw_zonal_inverse(jax.random.fold_in(key_list[9], 71), 0)
    meridional_inverse = draw_meridional_inverse(jax.random.fold_in(key_list[9], 71), 0)
    return dict(tide_state=tide_state, forcing=forcing, wet_mask=wet_mask, depth_band=depth_band, drag_table=drag_table, stiff_table=stiff_table, sample_times=sample_times, zonal_inverse=zonal_inverse, meridional_inverse=meridional_inverse)


TIDAL_FREQUENCIES = (0.5058680, 0.5235988, 0.4963657, 0.5250316, 0.2625162, 0.2433523, 0.2610812, 0.2338335)


def band_values(depth_band, lookup):
    values = jnp.zeros(depth_band.shape, jnp.float32)
    for band_level in range(lookup.shape[0]):
        values = values + jnp.where(depth_band == band_level, lookup[band_level], 0.0)
    return values


def sample_basis(sample_times, count):
    speeds = jnp.asarray(TIDAL_FREQUENCIES[:count], jnp.float32)
    phases = sample_times[:, None] * speeds[None, :]
    basis = jnp.stack([jnp.cos(phases), -jnp.sin(phases)], axis=2)
    return basis.reshape(sample_times.shape[0], 2 * count)


def friction_terms(flat_state, basis, drag_flat):
    velocity = jnp.dot(basis, flat_state, precision=lax.Precision.HIGHEST)
    stress = drag_flat[None, :] * jnp.abs(velocity) * velocity
    factor = 2.0 / basis.shape[0]
    return factor * lax.dot_general(basis, stress, (((0,), (0,)), ((), ())), precision=lax.Precision.HIGHEST)


def apply_operator(field, stiffness, turn_rates):
    padded = jnp.pad(field, ((0, 0), (0, 0), (1, 1), (0, 0)))
    neighbours = padded[:, :, 2:, :] + padded[:, :, :-2, :]
    neighbours = neighbours + jnp.roll(field, -1, axis=3) + jnp.roll(field, 1, axis=3)
    rotated = jnp.stack([-field[:, 1], field[:, 0]], axis=1)
    return 1.0 * field + turn_rates * rotated + stiffness * (4.0 * field - neighbours)


def reference(tide_state, forcing, wet_mask, depth_band, drag_table, stiff_table, sample_times, zonal_inverse, meridional_inverse):
    wet_cells = wet_mask.astype(jnp.float32)
    drag_cells = band_values(depth_band, drag_table)
    stiffness = band_values(depth_band, stiff_table)
    basis = sample_basis(sample_times, K)
    turn_rates = jnp.asarray(TIDAL_FREQUENCIES[:K], jnp.float32).reshape(K, 1, 1, 1)
    current = wet_cells * tide_state
    for sweep_index in range(ITERS):
        pieces = []
        for start_row in range(0, NY, LB):
            block_state = current[:, :, start_row:start_row + LB, :]
            flat_state = block_state.reshape(2 * K, -1)
            drag_flat = drag_cells[start_row:start_row + LB, :].reshape(-1)
            pieces.append(friction_terms(flat_state, basis, drag_flat).reshape(block_state.shape))
        friction = jnp.concatenate(pieces, axis=2)
        residual = wet_cells * (forcing - apply_operator(current, stiffness, turn_rates) - friction)
        blocks = residual.reshape(K, 2, NY, NX // LB, LB)
        zonal = jnp.einsum("kij,kprbj->kprbi", zonal_inverse, blocks, precision=lax.Precision.HIGHEST).reshape(residual.shape)
        blocks = zonal.reshape(K, 2, NY // LM, LM, NX)
        correction = jnp.einsum("kij,kpbjx->kpbix", meridional_inverse, blocks, precision=lax.Precision.HIGHEST).reshape(residual.shape)
        current = current + 0.25 * wet_cells * correction
    return current
```

```python
import functools

import jax
import jax.numpy as jnp
from jax import lax
from jax.experimental import pallas as pl
from jax.experimental.pallas import tpu as pltpu
from jax.sharding import PartitionSpec as P

MESH = pl.DeviceIdType.MESH
ITERS = 2
ROWS = 32
LANES = 128
COMPS = 16
SAMPLES = 48
RANKS = 16
CHIPS = 8
LM = 512

TIDAL_FREQUENCIES = (
    0.505868,
    0.5235988,
    0.4963657,
    0.5250316,
    0.2625162,
    0.2433523,
    0.2610812,
    0.2338335,
)

OFFSETS = [(dy, dc) for dy in (4, 3, 5, 2, 6, 1, 7) for dc in (0, 1)] + [(0, 1)]


def rotated_cosine(phase, quarter):
    turns = jnp.floor(phase * 0.63661977236758134308 + 0.5)
    rest = phase - turns * 1.5703125
    rest = rest - turns * 4.837512969970703125e-4
    rest = rest - turns * 7.54978995489188216e-8
    quadrant = (turns.astype(jnp.int32) + quarter) & 3
    square = rest * rest
    cosine = 1.0 + square * (
        -0.5 + square * (4.166664568298827e-2 + square * (-1.388731625493765e-3 + square * 2.443315711809948e-5))
    )
    sine = rest + rest * square * (
        -1.6666654611e-1 + square * (8.3321608736e-3 + square * -1.9515295891e-4)
    )
    value = jnp.where((quadrant & 1) == 1, -sine, cosine)
    return jnp.where(quadrant >= 2, -value, value)


def speeds_at(component):
    constituent = component >> 1
    speeds = jnp.zeros(component.shape, jnp.float32)
    for index, speed in enumerate(TIDAL_FREQUENCIES):
        speeds = jnp.where(constituent == index, jnp.float32(speed), speeds)
    return speeds


def high_part(value):
    return value.astype(jnp.bfloat16).astype(jnp.float32)


def split(value):
    high = value.astype(jnp.bfloat16)
    low = (value - high.astype(jnp.float32)).astype(jnp.bfloat16)
    return high, low


def iota(shape, dim):
    return lax.broadcasted_iota(jnp.int32, shape, dim)


def build_factors(times_ref, ahead_ref, back_ref):
    lane = iota((8, LANES), 1)
    row_times = jnp.zeros((8, LANES), jnp.float32)
    ahead_times = jnp.zeros((8, LANES), jnp.float32)
    for t in range(SAMPLES):
        value = times_ref[t]
        row_times = jnp.where((lane == 32 + t) | (lane == 80 + t), value, row_times)
        ahead_times = jnp.where((lane == t) | (lane == 48 + t), value, ahead_times)
    column_times = jnp.transpose(jnp.broadcast_to(ahead_times[0:1], (LANES, LANES)))[:96, :32]
    shape = (96, 32)
    col = iota(shape, 1)
    comp = col & 15
    value = rotated_cosine(column_times * speeds_at(comp), comp & 1)
    high = high_part(value)
    low = jnp.where(col < 16, value - high, 0.0)
    ahead_ref[...] = jnp.where(iota(shape, 0) < 48, high, low).astype(jnp.bfloat16)
    shape = (32, LANES)
    row, col = iota(shape, 0), iota(shape, 1)
    comp = row & 15
    speed = speeds_at(comp)
    times = jnp.broadcast_to(row_times[0:1], shape)
    basis = rotated_cosine(times * speed, comp & 1)
    other = col & 15
    turn = jnp.where(other == (comp ^ 1), jnp.where((comp & 1) == 0, -speed, speed), 0.0)
    value = jnp.where(col < 32, turn, basis)
    high = high_part(value)
    low_used = (col < 16) | ((col >= 32) & (col < 80))
    low = jnp.where(low_used, value - high, 0.0)
    back_ref[...] = jnp.where(row < 16, high, low).astype(jnp.bfloat16)


def kernel(
    tide_hbm, forcing_hbm, wet_hbm, band_hbm, drag_ref, stiff_ref, times_ref, zonal_hbm, meridional_hbm,
    out_ref,
    tide, forcing, wet_int, band, zonal_raw, mer_raw,
    wet, drag, stiff, ahead, back, zonal_w, mer_high, mer_low,
    cur, mix, back_terms, terms, edge_out, edge_in, row_in,
    fwd_out, fwd_in, ret_out, ret_in,
    local_sem, halo_send, halo_recv, fwd_send, fwd_recv, ret_send, ret_recv,
):
    samp = lax.axis_index("samp")
    space = lax.axis_index("space")
    n_samp = lax.axis_size("samp")
    n_space = lax.axis_size("space")
    rank = space % RANKS
    base = space - rank
    chip, core = rank // 2, rank % 2
    owned = rank // 2

    loads = [
        pltpu.make_async_copy(wet_hbm, wet_int, local_sem.at[0]),
        pltpu.make_async_copy(band_hbm, band, local_sem.at[1]),
        pltpu.make_async_copy(tide_hbm, tide, local_sem.at[2]),
        pltpu.make_async_copy(forcing_hbm, forcing, local_sem.at[3]),
        pltpu.make_async_copy(zonal_hbm.at[owned], zonal_raw, local_sem.at[4]),
        pltpu.make_async_copy(meridional_hbm.at[owned], mer_raw, local_sem.at[5]),
    ]
    for load in loads:
        load.start()

    north = {"space": (space + n_space - 1) % n_space}
    south = {"space": (space + 1) % n_space}
    west = {"samp": (samp + n_samp - 1) % n_samp}
    east = {"samp": (samp + 1) % n_samp}

    peers = []
    for dy, dc in OFFSETS:
        peers.append(((chip + dy) % CHIPS) * 2 + (core + dc) % 2)

    barrier = pltpu.get_barrier_semaphore()
    for target in [north, south, west, east] + [{"space": base + peer} for peer in peers]:
        pl.semaphore_signal(barrier, inc=1, device_id=target, device_id_type=MESH)

    build_factors(times_ref, ahead, back)

    loads[0].wait()
    loads[1].wait()
    wet[...] = wet_int[...].astype(jnp.float32)
    drags = jnp.zeros((ROWS, LANES), jnp.float32)
    stiffs = jnp.zeros((ROWS, LANES), jnp.float32)
    for level in range(drag_ref.shape[0]):
        here = band[...] == level
        drags = jnp.where(here, drag_ref[level], drags)
        stiffs = jnp.where(here, stiff_ref[level], stiffs)
    drag[...] = drags * (2.0 / SAMPLES)
    stiff[...] = stiffs

    tile = (COMPS, LANES)
    lane = iota(tile, 1)
    has_north = (space > 0).astype(jnp.float32)
    has_south = (space < n_space - 1).astype(jnp.float32)

    def shift(value, amount):
        amount = amount % LANES
        return value if amount == 0 else pltpu.roll(value, amount, 1)

    def set_state(it, r, value, edges):
        cur[it, comps(r), :] = value
        high, low = split(value)
        cols = pl.ds(r * LANES, LANES)
        mix[0:16, cols] = high
        mix[16:32, cols] = low
        first, last = edges
        first = jnp.where(lane == r, shift(value, r), first)
        last = jnp.where(lane == r, shift(value, r + 1), last)
        return first, last

    def comps(r):
        return pl.ds(r * COMPS, COMPS)

    def spread(ref, r):
        return jnp.broadcast_to(ref[pl.ds(r, 1), :], tile)

    def piece(rank_index):
        return pl.ds(pl.multiple_of(rank_index * ROWS, ROWS), ROWS)

    def exchange(it, source, target, send, recv):
        copies = []
        for peer in peers:
            copy = pltpu.make_async_remote_copy(
                src_ref=source.at[it, piece(peer), :],
                dst_ref=target.at[it, piece(rank), :],
                send_sem=send.at[it, peer],
                recv_sem=recv.at[it, rank],
                device_id={"space": base + peer},
                device_id_type=MESH,
            )
            copy.start()
            copies.append(copy)
        return copies

    def arrival(it, peer, source, target, send, recv):
        return pltpu.make_async_remote_copy(
            src_ref=source.at[it, piece(rank), :],
            dst_ref=target.at[it, piece(peer), :],
            send_sem=send.at[it, peer],
            recv_sem=recv.at[it, peer],
            device_id={"space": base + peer},
            device_id_type=MESH,
        )

    pending = []
    for it in range(ITERS):
        edges = (jnp.zeros(tile, jnp.float32), jnp.zeros(tile, jnp.float32))
        if it == 0:
            loads[2].wait()
            for r in range(ROWS):
                value = spread(wet, r) * tide[pl.ds(r, COMPS, stride=ROWS), :]
                edges = set_state(it, r, value, edges)
        else:
            for r in range(ROWS):
                step = ret_in[it - 1, pl.ds(r, COMPS, stride=ROWS), :]
                value = cur[it - 1, comps(r), :] + 0.25 * spread(wet, r) * step
                edges = set_state(it, r, value, edges)
        edge_out[it, 0] = edges[0]
        edge_out[it, 1] = edges[1]
        if it == 0:
            pl.semaphore_wait(barrier, 4 + len(peers))
        halos = []
        for slot, source, target, device in (
            (0, cur.at[it, comps(ROWS - 1), :], row_in.at[it, 0], south),
            (1, cur.at[it, comps(0), :], row_in.at[it, 1], north),
            (2, edge_out.at[it, 1], edge_in.at[it, 0], east),
            (3, edge_out.at[it, 0], edge_in.at[it, 1], west),
        ):
            copy = pltpu.make_async_remote_copy(
                src_ref=source,
                dst_ref=target,
                send_sem=halo_send.at[it, slot],
                recv_sem=halo_recv.at[it, slot],
                device_id=device,
                device_id_type=MESH,
            )
            copy.start()
            halos.append(copy)

        for start in range(0, ROWS, 4):
            cols = pl.ds(start * LANES, 4 * LANES)
            both = jnp.dot(ahead[...], mix[0:32, cols], preferred_element_type=jnp.float32)
            velocity = both[:SAMPLES] + both[SAMPLES:]
            for q in range(4):
                r = start + q
                part = velocity[:, q * LANES:(q + 1) * LANES]
                stress = jnp.broadcast_to(drag[pl.ds(r, 1), :], part.shape) * jnp.abs(part) * part
                high, low = split(stress)
                mix[32:80, pl.ds(r * LANES, LANES)] = high
                mix[80:128, pl.ds(r * LANES, LANES)] = low
            both = jnp.dot(back[...], mix[:, cols], preferred_element_type=jnp.float32)
            back_terms[:, cols] = both[:COMPS] + both[COMPS:]

        for copy in halos:
            copy.wait_recv()
        pending.extend(halos)
        west_in, east_in = edge_in[it, 0], edge_in[it, 1]
        for r in range(ROWS):
            value = cur[it, comps(r), :]
            up = cur[it, comps(r - 1), :] if r > 0 else row_in[it, 0] * has_north
            down = cur[it, comps(r + 1), :] if r < ROWS - 1 else row_in[it, 1] * has_south
            left = jnp.where(lane == 0, shift(west_in, LANES - r), shift(value, 1))
            right = jnp.where(lane == LANES - 1, shift(east_in, LANES - 1 - r), shift(value, LANES - 1))
            neighbours = (up + down) + (left + right)
            total = value + back_terms[:, pl.ds(r * LANES, LANES)] + spread(stiff, r) * (4.0 * value - neighbours)
            terms[comps(r), :] = total
        for c in range(COMPS):
            rows = pl.ds(c * ROWS, ROWS)
            fallen = terms[pl.ds(c, ROWS, stride=COMPS), :]
            if it == 0 and c == 0:
                loads[3].wait()
            fwd_out[it, rows, :] = wet[...] * (forcing[rows, :] - fallen)
        pending.extend(exchange(it, fwd_out, fwd_in, fwd_send, fwd_recv))
        fwd_in[it, piece(rank), :] = fwd_out[it, piece(rank), :]

        if it == 0:
            loads[4].wait()
            loads[5].wait()
            high, low = split(jnp.transpose(zonal_raw[...]))
            zonal_w[0:128, 0:128] = high
            zonal_w[0:128, 128:256] = low
            zonal_w[128:256, 0:128] = high
            zonal_w[128:256, 128:256] = jnp.zeros((LANES, LANES), jnp.bfloat16)
            for start in range(0, LM, 64):
                high, low = split(mer_raw[start:start + 64, :])
                mer_high[start:start + 64, :] = high
                mer_low[start:start + 64, :] = low

        for peer in peers:
            arrival(it, peer, fwd_out, fwd_in, fwd_send, fwd_recv).wait_recv()
        high, low = split(fwd_in[it])
        both = jnp.dot(jnp.concatenate([high, low], axis=1), zonal_w[...], preferred_element_type=jnp.float32)
        high, low = split(both[:, :LANES] + both[:, LANES:])
        both = jnp.dot(mer_high[...], jnp.concatenate([high, low], axis=1), preferred_element_type=jnp.float32)
        third = jnp.dot(mer_low[...], high, preferred_element_type=jnp.float32)
        ret_out[it] = both[:, :LANES] + both[:, LANES:] + third
        pending.extend(exchange(it, ret_out, ret_in, ret_send, ret_recv))
        ret_in[it, piece(rank), :] = ret_out[it, piece(rank), :]
        for peer in peers:
            arrival(it, peer, ret_out, ret_in, ret_send, ret_recv).wait_recv()

    last = ITERS - 1
    for c in range(COMPS):
        rows = pl.ds(c * ROWS, ROWS)
        state = cur[last, pl.ds(c, ROWS, stride=COMPS), :]
        out_ref[rows, :] = state + 0.25 * wet[...] * ret_in[last, rows, :]
    for copy in pending:
        copy.wait_send()


def body(
    tide_state,
    forcing,
    wet_mask,
    depth_band,
    drag_table,
    stiff_table,
    sample_times,
    zonal_inverse,
    meridional_inverse,
):
    flat = (COMPS * ROWS, LANES)
    f32, bf16 = jnp.float32, jnp.bfloat16
    dma = pltpu.SemaphoreType.DMA
    any_spec = pl.BlockSpec(memory_space=pl.ANY)
    smem = pl.BlockSpec(memory_space=pltpu.SMEM)
    result = pl.pallas_call(
        kernel,
        out_shape=jax.ShapeDtypeStruct(flat, f32),
        in_specs=[any_spec] * 4 + [smem] * 3 + [any_spec] * 2,
        out_specs=pl.BlockSpec(memory_space=pltpu.VMEM),
        scratch_shapes=[
            pltpu.VMEM(flat, f32),
            pltpu.VMEM(flat, f32),
            pltpu.VMEM((ROWS, LANES), jnp.int32),
            pltpu.VMEM((ROWS, LANES), jnp.int32),
            pltpu.VMEM((LANES, LANES), f32),
            pltpu.VMEM((LM, LM), f32),
            pltpu.VMEM((ROWS, LANES), f32),
            pltpu.VMEM((ROWS, LANES), f32),
            pltpu.VMEM((ROWS, LANES), f32),
            pltpu.VMEM((96, 32), bf16),
            pltpu.VMEM((32, LANES), bf16),
            pltpu.VMEM((256, 256), bf16),
            pltpu.VMEM((LM, LM), bf16),
            pltpu.VMEM((LM, LM), bf16),
            pltpu.VMEM((ITERS,) + flat, f32),
            pltpu.VMEM((LANES, ROWS * LANES), bf16),
            pltpu.VMEM((COMPS, ROWS * LANES), f32),
            pltpu.VMEM(flat, f32),
            pltpu.VMEM((ITERS, 2, COMPS, LANES), f32),
            pltpu.VMEM((ITERS, 2, COMPS, LANES), f32),
            pltpu.VMEM((ITERS, 2, COMPS, LANES), f32),
            pltpu.VMEM((ITERS,) + flat, f32),
            pltpu.VMEM((ITERS,) + flat, f32),
            pltpu.VMEM((ITERS,) + flat, f32),
            pltpu.VMEM((ITERS,) + flat, f32),
            dma((6,)),
            dma((ITERS, 4)),
            dma((ITERS, 4)),
            dma((ITERS, RANKS)),
            dma((ITERS, RANKS)),
            dma((ITERS, RANKS)),
            dma((ITERS, RANKS)),
        ],
        compiler_params=pltpu.CompilerParams(
            collective_id=0, has_side_effects=True, vmem_limit_bytes=40 * 1024 * 1024
        ),
        cost_estimate=pl.CostEstimate(flops=600000000, bytes_accessed=2500000, transcendentals=0),
    )(
        tide_state.reshape(flat),
        forcing.reshape(flat),
        wet_mask,
        depth_band,
        drag_table,
        stiff_table,
        sample_times,
        zonal_inverse,
        meridional_inverse,
    )
    return result.reshape(tide_state.shape)


def solution(mesh):
    grid = P(None, None, "space", "samp")
    return jax.shard_map(
        body,
        mesh=mesh,
        in_specs=(grid, grid, P("space", "samp"), P("space", "samp"), P(), P(), P(), P(), P()),
        out_specs=grid,
        check_vma=False,
    )
```

```python
import functools

import jax
import jax.numpy as jnp
from jax import lax
from jax.experimental import pallas as pl
from jax.experimental.pallas import tpu as pltpu
from jax.sharding import PartitionSpec as P

MESH = pl.DeviceIdType.MESH
ITERS = 2
ROWS = 32
LANES = 128
COMPS = 16
SAMPLES = 48
RANKS = 16
CHIPS = 8
LM = 512

TIDAL_FREQUENCIES = (
    0.505868,
    0.5235988,
    0.4963657,
    0.5250316,
    0.2625162,
    0.2433523,
    0.2610812,
    0.2338335,
)

OFFSETS = [(dy, dc) for dy in (4, 3, 5, 2, 6, 1, 7) for dc in (0, 1)] + [(0, 1)]


def rotated_cosine(phase, quarter):
    turns = jnp.floor(phase * 0.63661977236758134308 + 0.5)
    rest = phase - turns * 1.5703125
    rest = rest - turns * 4.837512969970703125e-4
    rest = rest - turns * 7.54978995489188216e-8
    quadrant = (turns.astype(jnp.int32) + quarter) & 3
    square = rest * rest
    cosine = 1.0 + square * (
        -0.5 + square * (4.166664568298827e-2 + square * (-1.388731625493765e-3 + square * 2.443315711809948e-5))
    )
    sine = rest + rest * square * (
        -1.6666654611e-1 + square * (8.3321608736e-3 + square * -1.9515295891e-4)
    )
    value = jnp.where((quadrant & 1) == 1, -sine, cosine)
    return jnp.where(quadrant >= 2, -value, value)


def speeds_at(component):
    constituent = component >> 1
    speeds = jnp.zeros(component.shape, jnp.float32)
    for index, speed in enumerate(TIDAL_FREQUENCIES):
        speeds = jnp.where(constituent == index, jnp.float32(speed), speeds)
    return speeds


def high_part(value):
    return value.astype(jnp.bfloat16).astype(jnp.float32)


def split(value):
    high = value.astype(jnp.bfloat16)
    low = (value - high.astype(jnp.float32)).astype(jnp.bfloat16)
    return high, low


def iota(shape, dim):
    return lax.broadcasted_iota(jnp.int32, shape, dim)


def build_factors(times_ref, ahead_ref, back_ref):
    lane = iota((8, LANES), 1)
    row_times = jnp.zeros((8, LANES), jnp.float32)
    ahead_times = jnp.zeros((8, LANES), jnp.float32)
    for t in range(SAMPLES):
        value = times_ref[t]
        row_times = jnp.where((lane == 32 + t) | (lane == 80 + t), value, row_times)
        ahead_times = jnp.where((lane == t) | (lane == 48 + t), value, ahead_times)
    column_times = jnp.transpose(jnp.broadcast_to(ahead_times[0:1], (LANES, LANES)))[:96, :32]
    shape = (96, 32)
    col = iota(shape, 1)
    comp = col & 15
    value = rotated_cosine(column_times * speeds_at(comp), comp & 1)
    high = high_part(value)
    low = jnp.where(col < 16, value - high, 0.0)
    ahead_ref[...] = jnp.where(iota(shape, 0) < 48, high, low).astype(jnp.bfloat16)
    shape = (32, LANES)
    row, col = iota(shape, 0), iota(shape, 1)
    comp = row & 15
    speed = speeds_at(comp)
    times = jnp.broadcast_to(row_times[0:1], shape)
    basis = rotated_cosine(times * speed, comp & 1)
    other = col & 15
    turn = jnp.where(other == (comp ^ 1), jnp.where((comp & 1) == 0, -speed, speed), 0.0)
    value = jnp.where(col < 32, turn, basis)
    high = high_part(value)
    low_used = (col < 16) | ((col >= 32) & (col < 80))
    low = jnp.where(low_used, value - high, 0.0)
    back_ref[...] = jnp.where(row < 16, high, low).astype(jnp.bfloat16)


def kernel(
    tide_hbm, forcing_hbm, wet_hbm, band_hbm, drag_ref, stiff_ref, times_ref, zonal_hbm, meridional_hbm,
    out_ref,
    tide, forcing, wet_int, band, zonal_raw, mer_raw,
    wet, drag, stiff, ahead, back, zonal_w, mer_high, mer_low,
    cur, mix, back_terms, terms, edge_out, edge_in, row_in,
    fwd_out, fwd_in, ret_out, ret_in,
    local_sem, halo_send, halo_recv, fwd_send, fwd_recv, ret_send, ret_recv,
):
    samp = lax.axis_index("samp")
    space = lax.axis_index("space")
    n_samp = lax.axis_size("samp")
    n_space = lax.axis_size("space")
    rank = space % RANKS
    base = space - rank
    chip, core = rank // 2, rank % 2
    owned = rank // 2

    loads = [
        pltpu.make_async_copy(wet_hbm, wet_int, local_sem.at[0]),
        pltpu.make_async_copy(band_hbm, band, local_sem.at[1]),
        pltpu.make_async_copy(tide_hbm, tide, local_sem.at[2]),
        pltpu.make_async_copy(forcing_hbm, forcing, local_sem.at[3]),
        pltpu.make_async_copy(zonal_hbm.at[owned], zonal_raw, local_sem.at[4]),
        pltpu.make_async_copy(meridional_hbm.at[owned], mer_raw, local_sem.at[5]),
    ]
    for load in loads:
        load.start()

    north = {"space": (space + n_space - 1) % n_space}
    south = {"space": (space + 1) % n_space}
    west = {"samp": (samp + n_samp - 1) % n_samp}
    east = {"samp": (samp + 1) % n_samp}

    peers = []
    for dy, dc in OFFSETS:
        peers.append(((chip + dy) % CHIPS) * 2 + (core + dc) % 2)

    barrier = pltpu.get_barrier_semaphore()
    for target in [north, south, west, east] + [{"space": base + peer} for peer in peers]:
        pl.semaphore_signal(barrier, inc=1, device_id=target, device_id_type=MESH)

    build_factors(times_ref, ahead, back)

    loads[0].wait()
    loads[1].wait()
    wet[...] = wet_int[...].astype(jnp.float32)
    drags = jnp.zeros((ROWS, LANES), jnp.float32)
    stiffs = jnp.zeros((ROWS, LANES), jnp.float32)
    for level in range(drag_ref.shape[0]):
        here = band[...] == level
        drags = jnp.where(here, drag_ref[level], drags)
        stiffs = jnp.where(here, stiff_ref[level], stiffs)
    drag[...] = drags * (2.0 / SAMPLES)
    stiff[...] = stiffs

    tile = (COMPS, LANES)
    lane = iota(tile, 1)
    has_north = (space > 0).astype(jnp.float32)
    has_south = (space < n_space - 1).astype(jnp.float32)

    def shift(value, amount):
        amount = amount % LANES
        return value if amount == 0 else pltpu.roll(value, amount, 1)

    def set_state(it, r, value, edges):
        cur[it, comps(r), :] = value
        high, low = split(value)
        cols = pl.ds(r * LANES, LANES)
        mix[0:16, cols] = high
        mix[16:32, cols] = low
        first, last = edges
        first = jnp.where(lane == r, shift(value, r), first)
        last = jnp.where(lane == r, shift(value, r + 1), last)
        return first, last

    def comps(r):
        return pl.ds(r * COMPS, COMPS)

    def spread(ref, r):
        return jnp.broadcast_to(ref[pl.ds(r, 1), :], tile)

    def piece(rank_index):
        return pl.ds(pl.multiple_of(rank_index * ROWS, ROWS), ROWS)

    def exchange(it, source, target, send, recv):
        copies = []
        for peer in peers:
            copy = pltpu.make_async_remote_copy(
                src_ref=source.at[it, piece(peer), :],
                dst_ref=target.at[it, piece(rank), :],
                send_sem=send.at[it, peer],
                recv_sem=recv.at[it, rank],
                device_id={"space": base + peer},
                device_id_type=MESH,
            )
            copy.start()
            copies.append(copy)
        return copies

    def arrival(it, peer, source, target, send, recv):
        return pltpu.make_async_remote_copy(
            src_ref=source.at[it, piece(rank), :],
            dst_ref=target.at[it, piece(peer), :],
            send_sem=send.at[it, peer],
            recv_sem=recv.at[it, peer],
            device_id={"space": base + peer},
            device_id_type=MESH,
        )

    def send_halos(it, halos):
        for slot, source, target, device in (
            (0, cur.at[it, comps(ROWS - 1), :], row_in.at[it, 0], south),
            (1, cur.at[it, comps(0), :], row_in.at[it, 1], north),
            (2, edge_out.at[it, 1], edge_in.at[it, 0], east),
            (3, edge_out.at[it, 0], edge_in.at[it, 1], west),
        ):
            copy = pltpu.make_async_remote_copy(
                src_ref=source,
                dst_ref=target,
                send_sem=halo_send.at[it, slot],
                recv_sem=halo_recv.at[it, slot],
                device_id=device,
                device_id_type=MESH,
            )
            copy.start()
            halos.append(copy)

    pending = []
    for it in range(ITERS):
        edges = (jnp.zeros(tile, jnp.float32), jnp.zeros(tile, jnp.float32))
        if it == 0:
            loads[2].wait()
            for r in range(ROWS):
                value = spread(wet, r) * tide[pl.ds(r, COMPS, stride=ROWS), :]
                edges = set_state(it, r, value, edges)
        else:
            for r in range(ROWS):
                step = ret_in[it - 1, pl.ds(r, COMPS, stride=ROWS), :]
                value = cur[it - 1, comps(r), :] + 0.25 * spread(wet, r) * step
                edges = set_state(it, r, value, edges)
        edge_out[it, 0] = edges[0]
        edge_out[it, 1] = edges[1]
        halos = []
        if it > 0:
            send_halos(it, halos)
        for start in range(0, ROWS, 4):
            cols = pl.ds(start * LANES, 4 * LANES)
            both = jnp.dot(ahead[...], mix[0:32, cols], preferred_element_type=jnp.float32)
            velocity = both[:SAMPLES] + both[SAMPLES:]
            for q in range(4):
                r = start + q
                part = velocity[:, q * LANES:(q + 1) * LANES]
                stress = jnp.broadcast_to(drag[pl.ds(r, 1), :], part.shape) * jnp.abs(part) * part
                high, low = split(stress)
                mix[32:80, pl.ds(r * LANES, LANES)] = high
                mix[80:128, pl.ds(r * LANES, LANES)] = low
            both = jnp.dot(back[...], mix[:, cols], preferred_element_type=jnp.float32)
            back_terms[:, cols] = both[:COMPS] + both[COMPS:]

        if it == 0:
            pl.semaphore_wait(barrier, 4 + len(peers))
            send_halos(it, halos)
        for copy in halos:
            copy.wait_recv()
        pending.extend(halos)
        west_in, east_in = edge_in[it, 0], edge_in[it, 1]
        for r in range(ROWS):
            value = cur[it, comps(r), :]
            up = cur[it, comps(r - 1), :] if r > 0 else row_in[it, 0] * has_north
            down = cur[it, comps(r + 1), :] if r < ROWS - 1 else row_in[it, 1] * has_south
            left = jnp.where(lane == 0, shift(west_in, LANES - r), shift(value, 1))
            right = jnp.where(lane == LANES - 1, shift(east_in, LANES - 1 - r), shift(value, LANES - 1))
            neighbours = (up + down) + (left + right)
            total = value + back_terms[:, pl.ds(r * LANES, LANES)] + spread(stiff, r) * (4.0 * value - neighbours)
            terms[comps(r), :] = total
        for c in range(COMPS):
            rows = pl.ds(c * ROWS, ROWS)
            fallen = terms[pl.ds(c, ROWS, stride=COMPS), :]
            if it == 0 and c == 0:
                loads[3].wait()
            fwd_out[it, rows, :] = wet[...] * (forcing[rows, :] - fallen)
        pending.extend(exchange(it, fwd_out, fwd_in, fwd_send, fwd_recv))
        fwd_in[it, piece(rank), :] = fwd_out[it, piece(rank), :]

        if it == 0:
            loads[4].wait()
            loads[5].wait()
            high, low = split(jnp.transpose(zonal_raw[...]))
            zonal_w[0:128, 0:128] = high
            zonal_w[0:128, 128:256] = low
            zonal_w[128:256, 0:128] = high
            zonal_w[128:256, 128:256] = jnp.zeros((LANES, LANES), jnp.bfloat16)
            for start in range(0, LM, 64):
                high, low = split(mer_raw[start:start + 64, :])
                mer_high[start:start + 64, :] = high
                mer_low[start:start + 64, :] = low

        for peer in peers:
            arrival(it, peer, fwd_out, fwd_in, fwd_send, fwd_recv).wait_recv()
        high, low = split(fwd_in[it])
        both = jnp.dot(jnp.concatenate([high, low], axis=1), zonal_w[...], preferred_element_type=jnp.float32)
        high, low = split(both[:, :LANES] + both[:, LANES:])
        both = jnp.dot(mer_high[...], jnp.concatenate([high, low], axis=1), preferred_element_type=jnp.float32)
        third = jnp.dot(mer_low[...], high, preferred_element_type=jnp.float32)
        ret_out[it] = both[:, :LANES] + both[:, LANES:] + third
        pending.extend(exchange(it, ret_out, ret_in, ret_send, ret_recv))
        ret_in[it, piece(rank), :] = ret_out[it, piece(rank), :]
        for peer in peers:
            arrival(it, peer, ret_out, ret_in, ret_send, ret_recv).wait_recv()

    last = ITERS - 1
    for c in range(COMPS):
        rows = pl.ds(c * ROWS, ROWS)
        state = cur[last, pl.ds(c, ROWS, stride=COMPS), :]
        out_ref[rows, :] = state + 0.25 * wet[...] * ret_in[last, rows, :]
    for copy in pending:
        copy.wait_send()


def body(
    tide_state,
    forcing,
    wet_mask,
    depth_band,
    drag_table,
    stiff_table,
    sample_times,
    zonal_inverse,
    meridional_inverse,
):
    flat = (COMPS * ROWS, LANES)
    f32, bf16 = jnp.float32, jnp.bfloat16
    dma = pltpu.SemaphoreType.DMA
    any_spec = pl.BlockSpec(memory_space=pltpu.HBM)
    smem = pl.BlockSpec(memory_space=pltpu.SMEM)
    result = pl.pallas_call(
        kernel,
        out_shape=jax.ShapeDtypeStruct(flat, f32),
        in_specs=[any_spec] * 4 + [smem] * 3 + [any_spec] * 2,
        out_specs=pl.BlockSpec(memory_space=pltpu.VMEM),
        scratch_shapes=[
            pltpu.VMEM(flat, f32),
            pltpu.VMEM(flat, f32),
            pltpu.VMEM((ROWS, LANES), jnp.int32),
            pltpu.VMEM((ROWS, LANES), jnp.int32),
            pltpu.VMEM((LANES, LANES), f32),
            pltpu.VMEM((LM, LM), f32),
            pltpu.VMEM((ROWS, LANES), f32),
            pltpu.VMEM((ROWS, LANES), f32),
            pltpu.VMEM((ROWS, LANES), f32),
            pltpu.VMEM((96, 32), bf16),
            pltpu.VMEM((32, LANES), bf16),
            pltpu.VMEM((256, 256), bf16),
            pltpu.VMEM((LM, LM), bf16),
            pltpu.VMEM((LM, LM), bf16),
            pltpu.VMEM((ITERS,) + flat, f32),
            pltpu.VMEM((LANES, ROWS * LANES), bf16),
            pltpu.VMEM((COMPS, ROWS * LANES), f32),
            pltpu.VMEM(flat, f32),
            pltpu.VMEM((ITERS, 2, COMPS, LANES), f32),
            pltpu.VMEM((ITERS, 2, COMPS, LANES), f32),
            pltpu.VMEM((ITERS, 2, COMPS, LANES), f32),
            pltpu.VMEM((ITERS,) + flat, f32),
            pltpu.VMEM((ITERS,) + flat, f32),
            pltpu.VMEM((ITERS,) + flat, f32),
            pltpu.VMEM((ITERS,) + flat, f32),
            dma((6,)),
            dma((ITERS, 4)),
            dma((ITERS, 4)),
            dma((ITERS, RANKS)),
            dma((ITERS, RANKS)),
            dma((ITERS, RANKS)),
            dma((ITERS, RANKS)),
        ],
        compiler_params=pltpu.CompilerParams(
            collective_id=0, has_side_effects=True, vmem_limit_bytes=64 * 1024 * 1024
        ),
        cost_estimate=pl.CostEstimate(flops=600000000, bytes_accessed=2500000, transcendentals=0),
    )(
        tide_state.reshape(flat),
        forcing.reshape(flat),
        wet_mask,
        depth_band,
        drag_table,
        stiff_table,
        sample_times,
        zonal_inverse,
        meridional_inverse,
    )
    return result.reshape(tide_state.shape)


def solution(mesh):
    grid = P(None, None, "space", "samp")
    return jax.shard_map(
        body,
        mesh=mesh,
        in_specs=(grid, grid, P("space", "samp"), P("space", "samp"), P(), P(), P(), P(), P()),
        out_specs=grid,
        check_vma=False,
    )
```

```python
import functools

import jax
import jax.numpy as jnp
from jax import lax
from jax.experimental import pallas as pl
from jax.experimental.pallas import tpu as pltpu
from jax.sharding import PartitionSpec as P

MESH = pl.DeviceIdType.MESH
ITERS = 2
ROWS = 32
LANES = 128
COMPS = 16
SAMPLES = 48
RANKS = 16
CHIPS = 8
LM = 512

TIDAL_FREQUENCIES = (
    0.505868,
    0.5235988,
    0.4963657,
    0.5250316,
    0.2625162,
    0.2433523,
    0.2610812,
    0.2338335,
)

OFFSETS = [(dy, dc) for dy in (4, 3, 5, 2, 6, 1, 7) for dc in (0, 1)] + [(0, 1)]


def rotated_cosine(phase, quarter):
    turns = jnp.floor(phase * 0.63661977236758134308 + 0.5)
    rest = phase - turns * 1.5703125
    rest = rest - turns * 4.837512969970703125e-4
    rest = rest - turns * 7.54978995489188216e-8
    quadrant = (turns.astype(jnp.int32) + quarter) & 3
    square = rest * rest
    cosine = 1.0 + square * (
        -0.5 + square * (4.166664568298827e-2 + square * (-1.388731625493765e-3 + square * 2.443315711809948e-5))
    )
    sine = rest + rest * square * (
        -1.6666654611e-1 + square * (8.3321608736e-3 + square * -1.9515295891e-4)
    )
    value = jnp.where((quadrant & 1) == 1, -sine, cosine)
    return jnp.where(quadrant >= 2, -value, value)


def speeds_at(component):
    constituent = component >> 1
    speeds = jnp.zeros(component.shape, jnp.float32)
    for index, speed in enumerate(TIDAL_FREQUENCIES):
        speeds = jnp.where(constituent == index, jnp.float32(speed), speeds)
    return speeds


def high_part(value):
    return value.astype(jnp.bfloat16).astype(jnp.float32)


def split(value):
    high = value.astype(jnp.bfloat16)
    low = (value - high.astype(jnp.float32)).astype(jnp.bfloat16)
    return high, low


def iota(shape, dim):
    return lax.broadcasted_iota(jnp.int32, shape, dim)


def build_factors(times_ref, ahead_ref, back_ref):
    lane = iota((8, LANES), 1)
    row_times = jnp.zeros((8, LANES), jnp.float32)
    ahead_times = jnp.zeros((8, LANES), jnp.float32)
    for t in range(SAMPLES):
        value = times_ref[t]
        row_times = jnp.where((lane == 32 + t) | (lane == 80 + t), value, row_times)
        ahead_times = jnp.where((lane == t) | (lane == 48 + t), value, ahead_times)
    column_times = jnp.transpose(jnp.broadcast_to(ahead_times[0:1], (LANES, LANES)))[:96, :32]
    shape = (96, 32)
    col = iota(shape, 1)
    comp = col & 15
    value = rotated_cosine(column_times * speeds_at(comp), comp & 1)
    high = high_part(value)
    low = jnp.where(col < 16, value - high, 0.0)
    ahead_ref[...] = jnp.where(iota(shape, 0) < 48, high, low).astype(jnp.bfloat16)
    shape = (32, LANES)
    row, col = iota(shape, 0), iota(shape, 1)
    comp = row & 15
    speed = speeds_at(comp)
    times = jnp.broadcast_to(row_times[0:1], shape)
    basis = rotated_cosine(times * speed, comp & 1)
    other = col & 15
    turn = jnp.where(other == (comp ^ 1), jnp.where((comp & 1) == 0, -speed, speed), 0.0)
    value = jnp.where(col < 32, turn, basis)
    high = high_part(value)
    low_used = (col < 16) | ((col >= 32) & (col < 80))
    low = jnp.where(low_used, value - high, 0.0)
    back_ref[...] = jnp.where(row < 16, high, low).astype(jnp.bfloat16)


def kernel(
    tide_hbm, forcing_hbm, wet_hbm, band_hbm, drag_ref, stiff_ref, times_ref, zonal_hbm, meridional_hbm,
    out_ref,
    tide, forcing, wet_int, band, zonal_raw, mer_raw,
    wet, drag, stiff, ahead, back, zonal_w, mer_high, mer_low,
    cur, mix, back_terms, terms, halo_out, halo_in, fix_out, fix_in, fix, end_out, end_in, zonal_lhs,
    fwd_out, fwd_in, ret_out, ret_in,
    local_sem, halo_send, halo_recv, fix_send, fix_recv, end_send, end_recv, fwd_send, fwd_recv, ret_send, ret_recv,
):
    samp = lax.axis_index("samp")
    space = lax.axis_index("space")
    n_samp = lax.axis_size("samp")
    n_space = lax.axis_size("space")
    rank = space % RANKS
    base = space - rank
    chip, core = rank // 2, rank % 2
    owned = rank // 2

    loads = [
        pltpu.make_async_copy(wet_hbm, wet_int, local_sem.at[0]),
        pltpu.make_async_copy(band_hbm, band, local_sem.at[1]),
        pltpu.make_async_copy(tide_hbm, tide, local_sem.at[2]),
        pltpu.make_async_copy(forcing_hbm, forcing, local_sem.at[3]),
        pltpu.make_async_copy(zonal_hbm.at[owned], zonal_raw, local_sem.at[4]),
        pltpu.make_async_copy(meridional_hbm.at[owned], mer_raw, local_sem.at[5]),
    ]
    for load in loads:
        load.start()

    north = {"space": (space + n_space - 1) % n_space}
    south = {"space": (space + 1) % n_space}
    west = {"samp": (samp + n_samp - 1) % n_samp}
    east = {"samp": (samp + 1) % n_samp}
    across = {"space": (space + RANKS) % n_space}

    peers = []
    for dy, dc in OFFSETS:
        peers.append(((chip + dy) % CHIPS) * 2 + (core + dc) % 2)

    barrier = pltpu.get_barrier_semaphore()
    for target in [north, south, west, east, across] + [{"space": base + peer} for peer in peers]:
        pl.semaphore_signal(barrier, inc=1, device_id=target, device_id_type=MESH)

    build_factors(times_ref, ahead, back)

    loads[0].wait()
    loads[1].wait()
    wet[...] = wet_int[...].astype(jnp.float32)
    drags = jnp.zeros((ROWS, LANES), jnp.float32)
    stiffs = jnp.zeros((ROWS, LANES), jnp.float32)
    for level in range(drag_ref.shape[0]):
        here = band[...] == level
        drags = jnp.where(here, drag_ref[level], drags)
        stiffs = jnp.where(here, stiff_ref[level], stiffs)
    drag[...] = drags * (2.0 / SAMPLES)
    stiff[...] = stiffs

    tile = (COMPS, LANES)
    lane = iota(tile, 1)
    block = (ROWS, LANES)
    block_row, block_lane = iota(block, 0), iota(block, 1)
    has_north = (space > 0).astype(jnp.float32)
    has_south = (space < n_space - 1).astype(jnp.float32)

    def shift(value, amount):
        amount = amount % LANES
        return value if amount == 0 else pltpu.roll(value, amount, 1)

    def comps(r):
        return pl.ds(r * COMPS, COMPS)

    def spread(ref, r):
        return jnp.broadcast_to(ref[pl.ds(r, 1), :], tile)

    def piece(rank_index, rows=ROWS):
        return pl.ds(pl.multiple_of(rank_index * rows, rows), rows)

    def columns_to_lanes(value, first_lane):
        picked = jnp.where(block_lane == block_row + first_lane, jnp.broadcast_to(value, block), 0.0)
        return picked

    def set_state(it, r, value):
        cur[it, comps(r), :] = value
        high, low = split(value)
        cols = pl.ds(r * LANES, LANES)
        mix[0:16, cols] = high
        mix[16:32, cols] = low

    def remote(source, target, send, recv, device):
        return pltpu.make_async_remote_copy(
            src_ref=source, dst_ref=target, send_sem=send, recv_sem=recv, device_id=device, device_id_type=MESH
        )

    def exchange(source, target, send, recv, rows):
        copies = []
        for peer in peers:
            copy = remote(
                source.at[piece(peer, rows), :], target.at[piece(rank, rows), :], send.at[peer], recv.at[rank],
                {"space": base + peer},
            )
            copy.start()
            copies.append(copy)
        target[piece(rank, rows), :] = source[piece(rank, rows), :]
        return copies

    def await_piece(peer, source, target, send, recv, rows):
        remote(
            source.at[piece(rank, rows), :], target.at[piece(peer, rows), :], send.at[peer], recv.at[peer],
            {"space": base + peer},
        ).wait_recv()

    def friction():
        for start in range(0, ROWS, 4):
            cols = pl.ds(start * LANES, 4 * LANES)
            both = jnp.dot(ahead[...], mix[0:32, cols], preferred_element_type=jnp.float32)
            velocity = both[:SAMPLES] + both[SAMPLES:]
            for q in range(4):
                r = start + q
                part = velocity[:, q * LANES:(q + 1) * LANES]
                stress = jnp.broadcast_to(drag[pl.ds(r, 1), :], part.shape) * jnp.abs(part) * part
                high, low = split(stress)
                mix[32:80, pl.ds(r * LANES, LANES)] = high
                mix[80:128, pl.ds(r * LANES, LANES)] = low
            both = jnp.dot(back[...], mix[:, cols], preferred_element_type=jnp.float32)
            back_terms[:, cols] = both[:COMPS] + both[COMPS:]

    def local_residual(it):
        for r in range(ROWS):
            value = cur[it, comps(r), :]
            left = jnp.where(lane == 0, 0.0, shift(value, 1))
            right = jnp.where(lane == LANES - 1, 0.0, shift(value, LANES - 1))
            neighbours = left + right
            if r > 0:
                neighbours = neighbours + cur[it, comps(r - 1), :]
            if r < ROWS - 1:
                neighbours = neighbours + cur[it, comps(r + 1), :]
            total = value + back_terms[:, pl.ds(r * LANES, LANES)] + spread(stiff, r) * (4.0 * value - neighbours)
            terms[comps(r), :] = total
        if it == 0:
            loads[3].wait()
        for c in range(COMPS):
            rows = pl.ds(c * ROWS, ROWS)
            fallen = terms[pl.ds(c, ROWS, stride=COMPS), :]
            fwd_out[it, rows, :] = wet[...] * (forcing[rows, :] - fallen)

    def edge_terms(owner, it):
        value = fwd_in[it, piece(owner), :]
        west_row = jnp.broadcast_to(fix[pl.ds(owner, 1), :], block)
        east_row = jnp.broadcast_to(fix[pl.ds(owner + RANKS, 1), :], block)
        north_row = jnp.broadcast_to(fix[pl.ds(owner + 2 * RANKS, 1), :], block)
        south_row = jnp.broadcast_to(fix[pl.ds(owner + 3 * RANKS, 1), :], block)
        same = block_lane == block_row
        west_col = jnp.sum(jnp.where(same, west_row, 0.0), axis=1, keepdims=True)
        east_col = jnp.sum(jnp.where(same, east_row, 0.0), axis=1, keepdims=True)
        value = value + jnp.where(block_lane == 0, west_col, 0.0) + jnp.where(block_lane == LANES - 1, east_col, 0.0)
        value = value + jnp.where(block_row == 0, north_row, 0.0) + jnp.where(block_row == ROWS - 1, south_row, 0.0)
        high, low = split(value)
        zonal_lhs[piece(owner), 0:LANES] = high
        zonal_lhs[piece(owner), LANES:2 * LANES] = low

    def solve(it):
        both = jnp.dot(zonal_lhs[...], zonal_w[...], preferred_element_type=jnp.float32)
        high, low = split(both[:, :LANES] + both[:, LANES:])
        both = jnp.dot(mer_high[...], jnp.concatenate([high, low], axis=1), preferred_element_type=jnp.float32)
        third = jnp.dot(mer_low[...], high, preferred_element_type=jnp.float32)
        ret_out[it] = both[:, :LANES] + both[:, LANES:] + third

    pending = []
    loads[2].wait()
    first = jnp.zeros(tile, jnp.float32)
    last = jnp.zeros(tile, jnp.float32)
    for r in range(ROWS):
        value = spread(wet, r) * tide[pl.ds(r, COMPS, stride=ROWS), :]
        set_state(0, r, value)
        first = jnp.where(lane == r, shift(value, r), first)
        last = jnp.where(lane == r, shift(value, r + 1), last)
    wets = wet[...]
    strength = wets * stiff[...]
    packed = jnp.sum(
        columns_to_lanes(wets[:, 0:1], 0)
        + columns_to_lanes(wets[:, LANES - 1:LANES], 32)
        + columns_to_lanes(strength[:, 0:1], 64)
        + columns_to_lanes(strength[:, LANES - 1:LANES], 96),
        axis=0,
        keepdims=True,
    )
    for slot, value, extra in (
        (0, cur[0, comps(ROWS - 1), :], wets[ROWS - 1:ROWS]),
        (1, cur[0, comps(0), :], wets[0:1]),
        (2, last, shift(packed, LANES - 32)),
        (3, first, packed),
    ):
        halo_out[slot, 0:COMPS, :] = value
        halo_out[slot, COMPS:COMPS + 8, :] = jnp.broadcast_to(extra, (8, LANES))
    friction()
    pl.semaphore_wait(barrier, 5 + len(peers))
    halos = []
    for slot, device in ((2, east), (3, west), (0, south), (1, north)):
        copy = remote(halo_out.at[slot], halo_in.at[slot], halo_send.at[slot], halo_recv.at[slot], device)
        copy.start()
        halos.append(copy)
    pending.extend(halos)
    local_residual(0)
    fwd = (fwd_out.at[0], fwd_in.at[0], fwd_send.at[0], fwd_recv.at[0], ROWS)
    pending.extend(exchange(*fwd))

    for copy in halos:
        copy.wait_recv()
    sides = (
        (2, shift(packed, 64)),
        (3, shift(packed, 32)),
        (0, strength[0:1] * has_north),
        (1, strength[ROWS - 1:ROWS] * has_south),
    )
    for j, (slot, factor) in enumerate(sides):
        factors = jnp.broadcast_to(factor, tile)
        near = jnp.broadcast_to(halo_in[slot, COMPS:COMPS + 1, :], tile)
        fix_out[pl.ds(j, COMPS, stride=8), :] = factors * halo_in[slot, 0:COMPS, :]
        fix_out[pl.ds(4 + j, COMPS, stride=8), :] = 0.25 * factors * near
    fixes = (fix_out, fix_in, fix_send, fix_recv, 8)
    pending.extend(exchange(*fixes))

    loads[4].wait()
    loads[5].wait()
    high, low = split(jnp.transpose(zonal_raw[...]))
    zonal_w[0:128, 0:128] = high
    zonal_w[0:128, 128:256] = low
    zonal_w[128:256, 0:128] = high
    zonal_w[128:256, 128:256] = jnp.zeros((LANES, LANES), jnp.bfloat16)
    for start in range(0, LM, 64):
        high, low = split(mer_raw[start:start + 64, :])
        mer_high[start:start + 64, :] = high
        mer_low[start:start + 64, :] = low

    for peer in peers:
        await_piece(peer, *fwd)
    for peer in peers:
        await_piece(peer, *fixes)
    for j in range(4):
        fix[j * RANKS:(j + 1) * RANKS, :] = fix_in[pl.ds(j, RANKS, stride=8), :]
    for owner in range(RANKS):
        edge_terms(owner, 0)
    solve(0)
    ret = (ret_out.at[0], ret_in.at[0], ret_send.at[0], ret_recv.at[0], ROWS)
    pending.extend(exchange(*ret))

    for owner in range(RANKS):
        value = ret_out[0, owner * ROWS:(owner + 1) * ROWS, :]
        end_out[owner:owner + 1, :] = jnp.sum(
            columns_to_lanes(value[:, 0:1], 0) + columns_to_lanes(value[:, LANES - 1:LANES], 32), axis=0, keepdims=True
        )
    end_out[16:17, :] = ret_out[0, 0:1, :]
    end_out[17:24, :] = jnp.broadcast_to(ret_out[0, LM - 1:LM, :], (7, LANES))
    ends = []
    for slot, device in ((0, east), (1, west), (2, across)):
        copy = remote(end_out, end_in.at[slot], end_send.at[slot], end_recv.at[slot], device)
        copy.start()
        ends.append(copy)
    pending.extend(ends)

    for peer in peers:
        await_piece(peer, *ret)
    for r in range(ROWS):
        step = ret_in[0, pl.ds(r, COMPS, stride=ROWS), :]
        set_state(1, r, cur[0, comps(r), :] + 0.25 * spread(wet, r) * step)
    friction()
    local_residual(1)
    fwd = (fwd_out.at[1], fwd_in.at[1], fwd_send.at[1], fwd_recv.at[1], ROWS)
    pending.extend(exchange(*fwd))

    for copy in ends:
        copy.wait_recv()
    norths = jnp.concatenate([end_in[2, 17:18, :], ret_out[0, pl.ds(ROWS - 1, RANKS, stride=ROWS), :][:RANKS - 1]], axis=0)
    souths = jnp.concatenate([ret_out[0, pl.ds(0, RANKS, stride=ROWS), :][1:], end_in[2, 16:17, :]], axis=0)
    steps = (shift(end_in[0, 0:RANKS, :], LANES - 32), end_in[1, 0:RANKS, :], norths, souths)
    for j, step in enumerate(steps):
        fix[j * RANKS:(j + 1) * RANKS, :] = (
            fix_in[pl.ds(j, RANKS, stride=8), :] + fix_in[pl.ds(4 + j, RANKS, stride=8), :] * step
        )
    edge_terms(rank, 1)
    for peer in peers[::-1]:
        await_piece(peer, *fwd)
        edge_terms(peer, 1)
    solve(1)
    ret = (ret_out.at[1], ret_in.at[1], ret_send.at[1], ret_recv.at[1], ROWS)
    pending.extend(exchange(*ret))
    for peer in peers:
        await_piece(peer, *ret)
    for c in range(COMPS):
        rows = pl.ds(c * ROWS, ROWS)
        state = cur[1, pl.ds(c, ROWS, stride=COMPS), :]
        out_ref[rows, :] = state + 0.25 * wet[...] * ret_in[1, rows, :]
    for copy in pending:
        copy.wait_send()


def body(
    tide_state,
    forcing,
    wet_mask,
    depth_band,
    drag_table,
    stiff_table,
    sample_times,
    zonal_inverse,
    meridional_inverse,
):
    flat = (COMPS * ROWS, LANES)
    f32, bf16 = jnp.float32, jnp.bfloat16
    dma = pltpu.SemaphoreType.DMA
    any_spec = pl.BlockSpec(memory_space=pltpu.HBM)
    smem = pl.BlockSpec(memory_space=pltpu.SMEM)
    result = pl.pallas_call(
        kernel,
        out_shape=jax.ShapeDtypeStruct(flat, f32),
        in_specs=[any_spec] * 4 + [smem] * 3 + [any_spec] * 2,
        out_specs=pl.BlockSpec(memory_space=pltpu.VMEM),
        scratch_shapes=[
            pltpu.VMEM(flat, f32),
            pltpu.VMEM(flat, f32),
            pltpu.VMEM((ROWS, LANES), jnp.int32),
            pltpu.VMEM((ROWS, LANES), jnp.int32),
            pltpu.VMEM((LANES, LANES), f32),
            pltpu.VMEM((LM, LM), f32),
            pltpu.VMEM((ROWS, LANES), f32),
            pltpu.VMEM((ROWS, LANES), f32),
            pltpu.VMEM((ROWS, LANES), f32),
            pltpu.VMEM((96, 32), bf16),
            pltpu.VMEM((32, LANES), bf16),
            pltpu.VMEM((256, 256), bf16),
            pltpu.VMEM((LM, LM), bf16),
            pltpu.VMEM((LM, LM), bf16),
            pltpu.VMEM((ITERS,) + flat, f32),
            pltpu.VMEM((LANES, ROWS * LANES), bf16),
            pltpu.VMEM((COMPS, ROWS * LANES), f32),
            pltpu.VMEM(flat, f32),
            pltpu.VMEM((4, COMPS + 8, LANES), f32),
            pltpu.VMEM((4, COMPS + 8, LANES), f32),
            pltpu.VMEM((8 * RANKS, LANES), f32),
            pltpu.VMEM((8 * RANKS, LANES), f32),
            pltpu.VMEM((4 * RANKS, LANES), f32),
            pltpu.VMEM((RANKS + 8, LANES), f32),
            pltpu.VMEM((3, RANKS + 8, LANES), f32),
            pltpu.VMEM((LM, 2 * LANES), bf16),
            pltpu.VMEM((ITERS,) + flat, f32),
            pltpu.VMEM((ITERS,) + flat, f32),
            pltpu.VMEM((ITERS,) + flat, f32),
            pltpu.VMEM((ITERS,) + flat, f32),
            dma((6,)),
            dma((4,)),
            dma((4,)),
            dma((RANKS,)),
            dma((RANKS,)),
            dma((3,)),
            dma((3,)),
            dma((ITERS, RANKS)),
            dma((ITERS, RANKS)),
            dma((ITERS, RANKS)),
            dma((ITERS, RANKS)),
        ],
        compiler_params=pltpu.CompilerParams(
            collective_id=0, has_side_effects=True, vmem_limit_bytes=64 * 1024 * 1024
        ),
        cost_estimate=pl.CostEstimate(flops=600000000, bytes_accessed=2500000, transcendentals=0),
    )(
        tide_state.reshape(flat),
        forcing.reshape(flat),
        wet_mask,
        depth_band,
        drag_table,
        stiff_table,
        sample_times,
        zonal_inverse,
        meridional_inverse,
    )
    return result.reshape(tide_state.shape)


def solution(mesh):
    grid = P(None, None, "space", "samp")
    return jax.shard_map(
        body,
        mesh=mesh,
        in_specs=(grid, grid, P("space", "samp"), P("space", "samp"), P(), P(), P(), P(), P()),
        out_specs=grid,
        check_vma=False,
    )
```

```python
import functools

import jax
import jax.numpy as jnp
from jax import lax
from jax.experimental import pallas as pl
from jax.experimental.pallas import tpu as pltpu
from jax.sharding import PartitionSpec as P

MESH = pl.DeviceIdType.MESH
ITERS = 2
ROWS = 32
HALF = 16
LANES = 128
COMPS = 16
SAMPLES = 48
RANKS = 16
CHIPS = 8
LM = 512

TIDAL_FREQUENCIES = (
    0.505868,
    0.5235988,
    0.4963657,
    0.5250316,
    0.2625162,
    0.2433523,
    0.2610812,
    0.2338335,
)

OFFSETS = [(dy, dc) for dy in (4, 3, 5, 2, 6, 1, 7) for dc in (0, 1)] + [(0, 1)]


def rotated_cosine(phase, quarter):
    turns = jnp.floor(phase * 0.63661977236758134308 + 0.5)
    rest = phase - turns * 1.5703125
    rest = rest - turns * 4.837512969970703125e-4
    rest = rest - turns * 7.54978995489188216e-8
    quadrant = (turns.astype(jnp.int32) + quarter) & 3
    square = rest * rest
    cosine = 1.0 + square * (
        -0.5 + square * (4.166664568298827e-2 + square * (-1.388731625493765e-3 + square * 2.443315711809948e-5))
    )
    sine = rest + rest * square * (
        -1.6666654611e-1 + square * (8.3321608736e-3 + square * -1.9515295891e-4)
    )
    value = jnp.where((quadrant & 1) == 1, -sine, cosine)
    return jnp.where(quadrant >= 2, -value, value)


def speeds_at(component):
    constituent = component >> 1
    speeds = jnp.zeros(component.shape, jnp.float32)
    for index, speed in enumerate(TIDAL_FREQUENCIES):
        speeds = jnp.where(constituent == index, jnp.float32(speed), speeds)
    return speeds


def high_part(value):
    return value.astype(jnp.bfloat16).astype(jnp.float32)


def split(value):
    high = value.astype(jnp.bfloat16)
    low = (value - high.astype(jnp.float32)).astype(jnp.bfloat16)
    return high, low


def iota(shape, dim):
    return lax.broadcasted_iota(jnp.int32, shape, dim)


def build_factors(times_ref, ahead_ref, back_ref):
    lane = iota((8, LANES), 1)
    row_times = jnp.zeros((8, LANES), jnp.float32)
    ahead_times = jnp.zeros((8, LANES), jnp.float32)
    for t in range(SAMPLES):
        value = times_ref[t]
        row_times = jnp.where((lane == 32 + t) | (lane == 80 + t), value, row_times)
        ahead_times = jnp.where((lane == t) | (lane == 48 + t), value, ahead_times)
    column_times = jnp.transpose(jnp.broadcast_to(ahead_times[0:1], (LANES, LANES)))[:96, :32]
    shape = (96, 32)
    col = iota(shape, 1)
    comp = col & 15
    value = rotated_cosine(column_times * speeds_at(comp), comp & 1)
    high = high_part(value)
    low = jnp.where(col < 16, value - high, 0.0)
    ahead_ref[...] = jnp.where(iota(shape, 0) < 48, high, low).astype(jnp.bfloat16)
    shape = (32, LANES)
    row, col = iota(shape, 0), iota(shape, 1)
    comp = row & 15
    speed = speeds_at(comp)
    times = jnp.broadcast_to(row_times[0:1], shape)
    basis = rotated_cosine(times * speed, comp & 1)
    other = col & 15
    turn = jnp.where(other == (comp ^ 1), jnp.where((comp & 1) == 0, -speed, speed), 0.0)
    value = jnp.where(col < 32, turn, basis)
    high = high_part(value)
    low_used = (col < 16) | ((col >= 32) & (col < 80))
    low = jnp.where(low_used, value - high, 0.0)
    back_ref[...] = jnp.where(row < 16, high, low).astype(jnp.bfloat16)


def kernel(
    tide_hbm, forcing_hbm, wet_hbm, band_hbm, drag_ref, stiff_ref, times_ref, zonal_hbm, meridional_hbm,
    out_ref,
    tide, forcing, wet_int, band, zonal_raw, mer_raw,
    wet, drag, stiff, ahead, back, zonal_w, mer_high, mer_low,
    cur, mix, back_terms, terms, halo_out, halo_in, fix_out, fix_in, fix, end_out, end_in, mid_out, mid_in, mid, zonal_lhs,
    fwd_out, fwd_in, ret_out, ret_in,
    local_sem, halo_send, halo_recv, fix_send, fix_recv, end_send, end_recv, mid_send, mid_recv, fwd_send, fwd_recv, ret_send, ret_recv,
):
    samp = lax.axis_index("samp")
    space = lax.axis_index("space")
    n_samp = lax.axis_size("samp")
    n_space = lax.axis_size("space")
    rank = space % RANKS
    base = space - rank
    chip, core = rank // 2, rank % 2
    owned = rank // 2

    loads = [
        pltpu.make_async_copy(wet_hbm, wet_int, local_sem.at[0]),
        pltpu.make_async_copy(band_hbm, band, local_sem.at[1]),
        pltpu.make_async_copy(tide_hbm, tide, local_sem.at[2]),
        pltpu.make_async_copy(forcing_hbm, forcing, local_sem.at[3]),
        pltpu.make_async_copy(zonal_hbm.at[owned], zonal_raw, local_sem.at[4]),
        pltpu.make_async_copy(meridional_hbm.at[owned], mer_raw, local_sem.at[5]),
    ]
    for load in loads:
        load.start()

    north = {"space": (space + n_space - 1) % n_space}
    south = {"space": (space + 1) % n_space}
    west = {"samp": (samp + n_samp - 1) % n_samp}
    east = {"samp": (samp + 1) % n_samp}
    across = {"space": (space + RANKS) % n_space}

    peers = []
    for dy, dc in OFFSETS:
        peers.append(((chip + dy) % CHIPS) * 2 + (core + dc) % 2)

    barrier = pltpu.get_barrier_semaphore()
    for target in [north, south, west, east, across] + [{"space": base + peer} for peer in peers]:
        pl.semaphore_signal(barrier, inc=1, device_id=target, device_id_type=MESH)

    build_factors(times_ref, ahead, back)

    loads[0].wait()
    loads[1].wait()
    wet[...] = wet_int[...].astype(jnp.float32)
    drags = jnp.zeros((ROWS, LANES), jnp.float32)
    stiffs = jnp.zeros((ROWS, LANES), jnp.float32)
    for level in range(drag_ref.shape[0]):
        here = band[...] == level
        drags = jnp.where(here, drag_ref[level], drags)
        stiffs = jnp.where(here, stiff_ref[level], stiffs)
    drag[...] = drags * (2.0 / SAMPLES)
    stiff[...] = stiffs

    tile = (COMPS, LANES)
    lane = iota(tile, 1)
    block = (ROWS, LANES)
    block_row, block_lane = iota(block, 0), iota(block, 1)
    has_north = (space > 0).astype(jnp.float32)
    has_south = (space < n_space - 1).astype(jnp.float32)

    def shift(value, amount):
        amount = amount % LANES
        return value if amount == 0 else pltpu.roll(value, amount, 1)

    def comps(r):
        return pl.ds(r * COMPS, COMPS)

    def spread(ref, r):
        return jnp.broadcast_to(ref[pl.ds(r, 1), :], tile)

    def piece(rank_index, rows=ROWS):
        return pl.ds(pl.multiple_of(rank_index * rows, rows), rows)

    def columns_to_lanes(value, first_lane):
        picked = jnp.where(block_lane == block_row + first_lane, jnp.broadcast_to(value, block), 0.0)
        return picked

    def set_state(it, r, value):
        cur[it, comps(r), :] = value
        high, low = split(value)
        cols = pl.ds(r * LANES, LANES)
        mix[0:16, cols] = high
        mix[16:32, cols] = low

    def remote(source, target, send, recv, device):
        return pltpu.make_async_remote_copy(
            src_ref=source, dst_ref=target, send_sem=send, recv_sem=recv, device_id=device, device_id_type=MESH
        )

    def exchange(source, target, send, recv, rows):
        copies = []
        for peer in peers:
            copy = remote(
                source.at[piece(peer, rows), :], target.at[piece(rank, rows), :], send.at[peer], recv.at[rank],
                {"space": base + peer},
            )
            copy.start()
            copies.append(copy)
        target[piece(rank, rows), :] = source[piece(rank, rows), :]
        return copies

    def await_piece(peer, source, target, send, recv, rows):
        remote(
            source.at[piece(rank, rows), :], target.at[piece(peer, rows), :], send.at[peer], recv.at[peer],
            {"space": base + peer},
        ).wait_recv()

    def exchange_half(half, source, target, send, recv, spot):
        copies = []
        for peer in peers:
            copy = remote(
                source.at[spot(half, peer), :], target.at[place(half, rank), :], send.at[half, peer],
                recv.at[half, rank], {"space": base + peer},
            )
            copy.start()
            copies.append(copy)
        target[place(half, rank), :] = source[spot(half, rank), :]
        return copies

    def await_half(half, peer, source, target, send, recv, spot):
        remote(
            source.at[spot(half, rank), :], target.at[place(half, peer), :], send.at[half, peer],
            recv.at[half, peer], {"space": base + peer},
        ).wait_recv()

    def place(half, rank_index):
        return pl.ds(pl.multiple_of(rank_index * ROWS + half * HALF, HALF), HALF)

    def solved(half, rank_index):
        return pl.ds(pl.multiple_of(half * RANKS * HALF + rank_index * HALF, HALF), HALF)

    def solved_rows(half, owner):
        return pl.ds(half * RANKS * HALF + owner * HALF, HALF)

    def friction(low_row=0, high_row=ROWS):
        for start in range(low_row, high_row, 4):
            cols = pl.ds(start * LANES, 4 * LANES)
            both = jnp.dot(ahead[...], mix[0:32, cols], preferred_element_type=jnp.float32)
            velocity = both[:SAMPLES] + both[SAMPLES:]
            for q in range(4):
                r = start + q
                part = velocity[:, q * LANES:(q + 1) * LANES]
                stress = jnp.broadcast_to(drag[pl.ds(r, 1), :], part.shape) * jnp.abs(part) * part
                high, low = split(stress)
                mix[32:80, pl.ds(r * LANES, LANES)] = high
                mix[80:128, pl.ds(r * LANES, LANES)] = low
            both = jnp.dot(back[...], mix[:, cols], preferred_element_type=jnp.float32)
            back_terms[:, cols] = both[:COMPS] + both[COMPS:]

    def local_terms(it, low_row, high_row):
        for r in range(low_row, high_row):
            value = cur[it, comps(r), :]
            left = jnp.where(lane == 0, 0.0, shift(value, 1))
            right = jnp.where(lane == LANES - 1, 0.0, shift(value, LANES - 1))
            neighbours = left + right
            if r > 0:
                neighbours = neighbours + cur[it, comps(r - 1), :]
            if r < high_row - 1:
                neighbours = neighbours + cur[it, comps(r + 1), :]
            total = value + back_terms[:, pl.ds(r * LANES, LANES)] + spread(stiff, r) * (4.0 * value - neighbours)
            terms[comps(r), :] = total

    def local_residual(it, low_row, high_row):
        count = high_row - low_row
        for c in range(COMPS):
            rows = pl.ds(c * ROWS + low_row, count)
            fallen = terms[pl.ds(low_row * COMPS + c, count, stride=COMPS), :]
            fwd_out[it, rows, :] = wet[low_row:high_row] * (forcing[rows, :] - fallen)

    def edge_terms(owner, it):
        value = fwd_in[it, piece(owner), :]
        west_row = jnp.broadcast_to(fix[pl.ds(owner, 1), :], block)
        east_row = jnp.broadcast_to(fix[pl.ds(owner + RANKS, 1), :], block)
        north_row = jnp.broadcast_to(fix[pl.ds(owner + 2 * RANKS, 1), :], block)
        south_row = jnp.broadcast_to(fix[pl.ds(owner + 3 * RANKS, 1), :], block)
        same = block_lane == block_row
        west_col = jnp.sum(jnp.where(same, west_row, 0.0), axis=1, keepdims=True)
        east_col = jnp.sum(jnp.where(same, east_row, 0.0), axis=1, keepdims=True)
        value = value + jnp.where(block_lane == 0, west_col, 0.0) + jnp.where(block_lane == LANES - 1, east_col, 0.0)
        value = value + jnp.where(block_row == 0, north_row, 0.0) + jnp.where(block_row == ROWS - 1, south_row, 0.0)
        if it == 1:
            mid_row = jnp.broadcast_to(mid[pl.ds(owner, 1), :], block)
            value = value + jnp.where(block_row == HALF - 1, mid_row, 0.0)
        high, low = split(value)
        zonal_lhs[piece(owner), 0:LANES] = high
        zonal_lhs[piece(owner), LANES:2 * LANES] = low

    def solve(it):
        both = jnp.dot(zonal_lhs[...], zonal_w[...], preferred_element_type=jnp.float32)
        high, low = split(both[:, :LANES] + both[:, LANES:])
        pair = jnp.concatenate([high, low], axis=1)
        copies = []
        for half in range(2):
            rows = pl.ds(half * RANKS * HALF, RANKS * HALF)
            both = jnp.dot(mer_high[rows, :], pair, preferred_element_type=jnp.float32)
            third = jnp.dot(mer_low[rows, :], high, preferred_element_type=jnp.float32)
            ret_out[it, rows, :] = both[:, :LANES] + both[:, LANES:] + third
            copies.extend(exchange_half(half, *returns(it)))
        return copies

    def returns(it):
        return ret_out.at[it], ret_in.at[it], ret_send.at[it], ret_recv.at[it], solved

    pending = []
    loads[2].wait()
    first = jnp.zeros(tile, jnp.float32)
    last = jnp.zeros(tile, jnp.float32)
    for r in range(ROWS):
        value = spread(wet, r) * tide[pl.ds(r, COMPS, stride=ROWS), :]
        set_state(0, r, value)
        first = jnp.where(lane == r, shift(value, r), first)
        last = jnp.where(lane == r, shift(value, r + 1), last)
    wets = wet[...]
    strength = wets * stiff[...]
    packed = jnp.sum(
        columns_to_lanes(wets[:, 0:1], 0)
        + columns_to_lanes(wets[:, LANES - 1:LANES], 32)
        + columns_to_lanes(strength[:, 0:1], 64)
        + columns_to_lanes(strength[:, LANES - 1:LANES], 96),
        axis=0,
        keepdims=True,
    )
    for slot, value, extra in (
        (0, cur[0, comps(ROWS - 1), :], wets[ROWS - 1:ROWS]),
        (1, cur[0, comps(0), :], wets[0:1]),
        (2, last, shift(packed, LANES - 32)),
        (3, first, packed),
    ):
        halo_out[slot, 0:COMPS, :] = value
        halo_out[slot, COMPS:COMPS + 8, :] = jnp.broadcast_to(extra, (8, LANES))
    friction()
    pl.semaphore_wait(barrier, 5 + len(peers))
    halos = []
    for slot, device in ((2, east), (3, west), (0, south), (1, north)):
        copy = remote(halo_out.at[slot], halo_in.at[slot], halo_send.at[slot], halo_recv.at[slot], device)
        copy.start()
        halos.append(copy)
    pending.extend(halos)
    local_terms(0, 0, ROWS)
    loads[3].wait()
    local_residual(0, 0, ROWS)
    fwd = (fwd_out.at[0], fwd_in.at[0], fwd_send.at[0, 0], fwd_recv.at[0, 0], ROWS)
    pending.extend(exchange(*fwd))

    for copy in halos:
        copy.wait_recv()
    sides = (
        (2, shift(packed, 64)),
        (3, shift(packed, 32)),
        (0, strength[0:1] * has_north),
        (1, strength[ROWS - 1:ROWS] * has_south),
    )
    for j, (slot, factor) in enumerate(sides):
        factors = jnp.broadcast_to(factor, tile)
        near = jnp.broadcast_to(halo_in[slot, COMPS:COMPS + 1, :], tile)
        fix_out[pl.ds(j, COMPS, stride=8), :] = factors * halo_in[slot, 0:COMPS, :]
        fix_out[pl.ds(4 + j, COMPS, stride=8), :] = 0.25 * factors * near
    fixes = (fix_out, fix_in, fix_send, fix_recv, 8)
    pending.extend(exchange(*fixes))
    factors = jnp.broadcast_to(strength[HALF - 1:HALF], tile)
    mid_out[pl.ds(0, COMPS, stride=8), :] = factors * cur[0, comps(HALF), :]
    mid_out[pl.ds(1, COMPS, stride=8), :] = 0.25 * factors * jnp.broadcast_to(wets[HALF:HALF + 1], tile)
    for j in range(2, 8):
        mid_out[pl.ds(j, COMPS, stride=8), :] = jnp.zeros(tile, jnp.float32)
    mids = (mid_out, mid_in, mid_send, mid_recv, 8)
    pending.extend(exchange(*mids))

    loads[4].wait()
    loads[5].wait()
    high, low = split(jnp.transpose(zonal_raw[...]))
    zonal_w[0:128, 0:128] = high
    zonal_w[0:128, 128:256] = low
    zonal_w[128:256, 0:128] = high
    zonal_w[128:256, 128:256] = jnp.zeros((LANES, LANES), jnp.bfloat16)
    for owner in range(RANKS):
        for half in range(2):
            start = owner * ROWS + half * HALF
            high, low = split(mer_raw[start:start + HALF, :])
            mer_high[solved_rows(half, owner), :] = high
            mer_low[solved_rows(half, owner), :] = low

    for peer in peers:
        await_piece(peer, *fwd)
    for peer in peers:
        await_piece(peer, *fixes)
    for j in range(4):
        fix[j * RANKS:(j + 1) * RANKS, :] = fix_in[pl.ds(j, RANKS, stride=8), :]
    for owner in range(RANKS):
        edge_terms(owner, 0)
    pending.extend(solve(0))

    for owner in range(RANKS):
        value = jnp.concatenate([ret_out[0, solved_rows(0, owner), :], ret_out[0, solved_rows(1, owner), :]], axis=0)
        end_out[owner:owner + 1, :] = jnp.sum(
            columns_to_lanes(value[:, 0:1], 0) + columns_to_lanes(value[:, LANES - 1:LANES], 32), axis=0, keepdims=True
        )
    end_out[16:17, :] = ret_out[0, 0:1, :]
    end_out[17:24, :] = jnp.broadcast_to(ret_out[0, LM - 1:LM, :], (7, LANES))
    ends = []
    for slot, device in ((0, east), (1, west), (2, across)):
        copy = remote(end_out, end_in.at[slot], end_send.at[slot], end_recv.at[slot], device)
        copy.start()
        ends.append(copy)
    pending.extend(ends)

    for half in range(2):
        for peer in peers:
            await_half(half, peer, *returns(0))
        low_row, high_row = half * HALF, (half + 1) * HALF
        for r in range(low_row, high_row):
            step = ret_in[0, pl.ds(r, COMPS, stride=ROWS), :]
            set_state(1, r, cur[0, comps(r), :] + 0.25 * spread(wet, r) * step)
        friction(low_row, high_row)
        local_terms(1, low_row, high_row)
        local_residual(1, low_row, high_row)
        pending.extend(exchange_half(half, fwd_out.at[1], fwd_in.at[1], fwd_send.at[1], fwd_recv.at[1], place))

    for peer in peers:
        await_piece(peer, *mids)
    for copy in ends:
        copy.wait_recv()
    norths = jnp.concatenate([end_in[2, 17:18, :], ret_out[0, pl.ds(RANKS * HALF + HALF - 1, RANKS, stride=HALF), :][:RANKS - 1]], axis=0)
    souths = jnp.concatenate([ret_out[0, pl.ds(0, RANKS, stride=HALF), :][1:], end_in[2, 16:17, :]], axis=0)
    steps = (shift(end_in[0, 0:RANKS, :], LANES - 32), end_in[1, 0:RANKS, :], norths, souths)
    for j, step in enumerate(steps):
        fix[j * RANKS:(j + 1) * RANKS, :] = (
            fix_in[pl.ds(j, RANKS, stride=8), :] + fix_in[pl.ds(4 + j, RANKS, stride=8), :] * step
        )
    mid[...] = mid_in[pl.ds(0, RANKS, stride=8), :] + mid_in[pl.ds(1, RANKS, stride=8), :] * ret_out[
        0, pl.ds(RANKS * HALF, RANKS, stride=HALF), :
    ]
    edge_terms(rank, 1)
    for peer in peers[::-1]:
        for half in range(2):
            await_half(half, peer, fwd_out.at[1], fwd_in.at[1], fwd_send.at[1], fwd_recv.at[1], place)
        edge_terms(peer, 1)
    pending.extend(solve(1))
    for half in range(2):
        for peer in peers:
            await_half(half, peer, *returns(1))
        for c in range(COMPS):
            rows = pl.ds(c * ROWS + half * HALF, HALF)
            state = cur[1, pl.ds(half * HALF * COMPS + c, HALF, stride=COMPS), :]
            out_ref[rows, :] = state + 0.25 * wet[half * HALF:(half + 1) * HALF] * ret_in[1, rows, :]
    for copy in pending:
        copy.wait_send()


def body(
    tide_state,
    forcing,
    wet_mask,
    depth_band,
    drag_table,
    stiff_table,
    sample_times,
    zonal_inverse,
    meridional_inverse,
):
    flat = (COMPS * ROWS, LANES)
    f32, bf16 = jnp.float32, jnp.bfloat16
    dma = pltpu.SemaphoreType.DMA
    any_spec = pl.BlockSpec(memory_space=pltpu.HBM)
    smem = pl.BlockSpec(memory_space=pltpu.SMEM)
    result = pl.pallas_call(
        kernel,
        out_shape=pltpu.VMEM(flat, f32),
        in_specs=[any_spec] * 4 + [smem] * 3 + [any_spec] * 2,
        out_specs=pl.BlockSpec(memory_space=pltpu.VMEM),
        scratch_shapes=[
            pltpu.VMEM(flat, f32),
            pltpu.VMEM(flat, f32),
            pltpu.VMEM((ROWS, LANES), jnp.int32),
            pltpu.VMEM((ROWS, LANES), jnp.int32),
            pltpu.VMEM((LANES, LANES), f32),
            pltpu.VMEM((LM, LM), f32),
            pltpu.VMEM((ROWS, LANES), f32),
            pltpu.VMEM((ROWS, LANES), f32),
            pltpu.VMEM((ROWS, LANES), f32),
            pltpu.VMEM((96, 32), bf16),
            pltpu.VMEM((32, LANES), bf16),
            pltpu.VMEM((256, 256), bf16),
            pltpu.VMEM((LM, LM), bf16),
            pltpu.VMEM((LM, LM), bf16),
            pltpu.VMEM((ITERS,) + flat, f32),
            pltpu.VMEM((LANES, ROWS * LANES), bf16),
            pltpu.VMEM((COMPS, ROWS * LANES), f32),
            pltpu.VMEM(flat, f32),
            pltpu.VMEM((4, COMPS + 8, LANES), f32),
            pltpu.VMEM((4, COMPS + 8, LANES), f32),
            pltpu.VMEM((8 * RANKS, LANES), f32),
            pltpu.VMEM((8 * RANKS, LANES), f32),
            pltpu.VMEM((4 * RANKS, LANES), f32),
            pltpu.VMEM((RANKS + 8, LANES), f32),
            pltpu.VMEM((3, RANKS + 8, LANES), f32),
            pltpu.VMEM((8 * RANKS, LANES), f32),
            pltpu.VMEM((8 * RANKS, LANES), f32),
            pltpu.VMEM((RANKS, LANES), f32),
            pltpu.VMEM((LM, 2 * LANES), bf16),
            pltpu.VMEM((ITERS,) + flat, f32),
            pltpu.VMEM((ITERS,) + flat, f32),
            pltpu.VMEM((ITERS,) + flat, f32),
            pltpu.VMEM((ITERS,) + flat, f32),
            dma((6,)),
            dma((4,)),
            dma((4,)),
            dma((RANKS,)),
            dma((RANKS,)),
            dma((3,)),
            dma((3,)),
            dma((RANKS,)),
            dma((RANKS,)),
            dma((ITERS, 2, RANKS)),
            dma((ITERS, 2, RANKS)),
            dma((ITERS, 2, RANKS)),
            dma((ITERS, 2, RANKS)),
        ],
        compiler_params=pltpu.CompilerParams(
            collective_id=0, has_side_effects=True, vmem_limit_bytes=60 * 1024 * 1024
        ),
        cost_estimate=pl.CostEstimate(flops=600000000, bytes_accessed=2500000, transcendentals=0),
    )(
        tide_state.reshape(flat),
        forcing.reshape(flat),
        wet_mask,
        depth_band,
        drag_table,
        stiff_table,
        sample_times,
        zonal_inverse,
        meridional_inverse,
    )
    return result.reshape(tide_state.shape)


def solution(mesh):
    grid = P(None, None, "space", "samp")
    return jax.shard_map(
        body,
        mesh=mesh,
        in_specs=(grid, grid, P("space", "samp"), P("space", "samp"), P(), P(), P(), P(), P()),
        out_specs=grid,
        check_vma=False,
    )
```

```python
import functools

import jax
import jax.numpy as jnp
from jax import lax
from jax.experimental import pallas as pl
from jax.experimental.pallas import tpu as pltpu
from jax.sharding import PartitionSpec as P

MESH = pl.DeviceIdType.MESH
ITERS = 2
ROWS = 32
HALF = 16
LANES = 128
COMPS = 16
SAMPLES = 48
RANKS = 16
CHIPS = 8
LM = 512

TIDAL_FREQUENCIES = (
    0.505868,
    0.5235988,
    0.4963657,
    0.5250316,
    0.2625162,
    0.2433523,
    0.2610812,
    0.2338335,
)

OFFSETS = [(dy, dc) for dy in (4, 3, 5, 2, 6, 1, 7) for dc in (0, 1)] + [(0, 1)]


def rotated_cosine(phase, quarter):
    turns = jnp.floor(phase * 0.63661977236758134308 + 0.5)
    rest = phase - turns * 1.5703125
    rest = rest - turns * 4.837512969970703125e-4
    rest = rest - turns * 7.54978995489188216e-8
    quadrant = (turns.astype(jnp.int32) + quarter) & 3
    square = rest * rest
    cosine = 1.0 + square * (
        -0.5 + square * (4.166664568298827e-2 + square * (-1.388731625493765e-3 + square * 2.443315711809948e-5))
    )
    sine = rest + rest * square * (
        -1.6666654611e-1 + square * (8.3321608736e-3 + square * -1.9515295891e-4)
    )
    value = jnp.where((quadrant & 1) == 1, -sine, cosine)
    return jnp.where(quadrant >= 2, -value, value)


def speeds_at(component):
    constituent = component >> 1
    speeds = jnp.zeros(component.shape, jnp.float32)
    for index, speed in enumerate(TIDAL_FREQUENCIES):
        speeds = jnp.where(constituent == index, jnp.float32(speed), speeds)
    return speeds


def high_part(value):
    return value.astype(jnp.bfloat16).astype(jnp.float32)


def split(value):
    high = value.astype(jnp.bfloat16)
    low = (value - high.astype(jnp.float32)).astype(jnp.bfloat16)
    return high, low


def iota(shape, dim):
    return lax.broadcasted_iota(jnp.int32, shape, dim)


def build_factors(times_ref, ahead_ref, back_ref):
    lane = iota((8, LANES), 1)
    row_times = jnp.zeros((8, LANES), jnp.float32)
    ahead_times = jnp.zeros((8, LANES), jnp.float32)
    for t in range(SAMPLES):
        value = times_ref[t]
        row_times = jnp.where((lane == 32 + t) | (lane == 80 + t), value, row_times)
        ahead_times = jnp.where((lane == t) | (lane == 48 + t), value, ahead_times)
    column_times = jnp.transpose(jnp.broadcast_to(ahead_times[0:1], (LANES, LANES)))[:96, :32]
    shape = (96, 32)
    col = iota(shape, 1)
    comp = col & 15
    value = rotated_cosine(column_times * speeds_at(comp), comp & 1)
    high = high_part(value)
    low = jnp.where(col < 16, value - high, 0.0)
    ahead_ref[...] = jnp.where(iota(shape, 0) < 48, high, low).astype(jnp.bfloat16)
    shape = (32, LANES)
    row, col = iota(shape, 0), iota(shape, 1)
    comp = row & 15
    speed = speeds_at(comp)
    times = jnp.broadcast_to(row_times[0:1], shape)
    basis = rotated_cosine(times * speed, comp & 1)
    other = col & 15
    turn = jnp.where(other == (comp ^ 1), jnp.where((comp & 1) == 0, -speed, speed), 0.0)
    value = jnp.where(col < 32, turn, basis)
    high = high_part(value)
    low_used = (col < 16) | ((col >= 32) & (col < 80))
    low = jnp.where(low_used, value - high, 0.0)
    back_ref[...] = jnp.where(row < 16, high, low).astype(jnp.bfloat16)


def kernel(
    tide_hbm, forcing_hbm, wet_hbm, band_hbm, drag_ref, stiff_ref, times_ref, zonal_hbm, meridional_hbm,
    out_ref,
    tide, forcing, wet_int, band, zonal_raw, mer_raw,
    wet, drag, stiff, ahead, back, zonal_w, mer_high, mer_low,
    cur, mix, back_terms, terms, halo_out, halo_in, fix_out, fix_in, fix, end_out, end_in, rim_out, rim_in, far, late_out, late_in, full, shape_w, shape_e, mid, zonal_lhs,
    fwd_out, fwd_in, ret_out, ret_in,
    local_sem, halo_send, halo_recv, fix_send, fix_recv, end_send, end_recv, rim_send, rim_recv, late_send, late_recv, fwd_send, fwd_recv, ret_send, ret_recv,
):
    samp = lax.axis_index("samp")
    space = lax.axis_index("space")
    n_samp = lax.axis_size("samp")
    n_space = lax.axis_size("space")
    rank = space % RANKS
    base = space - rank
    chip, core = rank // 2, rank % 2
    owned = rank // 2

    loads = [
        pltpu.make_async_copy(wet_hbm, wet_int, local_sem.at[0]),
        pltpu.make_async_copy(band_hbm, band, local_sem.at[1]),
        pltpu.make_async_copy(tide_hbm, tide, local_sem.at[2]),
        pltpu.make_async_copy(forcing_hbm, forcing, local_sem.at[3]),
        pltpu.make_async_copy(zonal_hbm, zonal_raw, local_sem.at[4]),
        pltpu.make_async_copy(meridional_hbm.at[owned], mer_raw, local_sem.at[5]),
    ]
    for load in loads:
        load.start()

    north = {"space": (space + n_space - 1) % n_space}
    south = {"space": (space + 1) % n_space}
    west = {"samp": (samp + n_samp - 1) % n_samp}
    east = {"samp": (samp + 1) % n_samp}
    across = {"space": (space + RANKS) % n_space}

    peers = []
    for dy, dc in OFFSETS:
        peers.append(((chip + dy) % CHIPS) * 2 + (core + dc) % 2)

    barrier = pltpu.get_barrier_semaphore()
    for target in [north, south, west, east, across] + [{"space": base + peer} for peer in peers]:
        pl.semaphore_signal(barrier, inc=1, device_id=target, device_id_type=MESH)

    build_factors(times_ref, ahead, back)

    loads[0].wait()
    loads[1].wait()
    wet[...] = wet_int[...].astype(jnp.float32)
    drags = jnp.zeros((ROWS, LANES), jnp.float32)
    stiffs = jnp.zeros((ROWS, LANES), jnp.float32)
    for level in range(drag_ref.shape[0]):
        here = band[...] == level
        drags = jnp.where(here, drag_ref[level], drags)
        stiffs = jnp.where(here, stiff_ref[level], stiffs)
    drag[...] = drags * (2.0 / SAMPLES)
    stiff[...] = stiffs

    tile = (COMPS, LANES)
    lane = iota(tile, 1)
    block = (ROWS, LANES)
    block_row, block_lane = iota(block, 0), iota(block, 1)
    has_north = (space > 0).astype(jnp.float32)
    has_south = (space < n_space - 1).astype(jnp.float32)

    def shift(value, amount):
        amount = amount % LANES
        return value if amount == 0 else pltpu.roll(value, amount, 1)

    def comps(r):
        return pl.ds(r * COMPS, COMPS)

    def spread(ref, r):
        return jnp.broadcast_to(ref[pl.ds(r, 1), :], tile)

    def piece(rank_index, rows=ROWS):
        return pl.ds(pl.multiple_of(rank_index * rows, rows), rows)

    def columns_to_lanes(value, first_lane):
        picked = jnp.where(block_lane == block_row + first_lane, jnp.broadcast_to(value, block), 0.0)
        return picked

    def set_state(it, r, value):
        cur[it, comps(r), :] = value
        high, low = split(value)
        cols = pl.ds(r * LANES, LANES)
        mix[0:16, cols] = high
        mix[16:32, cols] = low

    def remote(source, target, send, recv, device):
        return pltpu.make_async_remote_copy(
            src_ref=source, dst_ref=target, send_sem=send, recv_sem=recv, device_id=device, device_id_type=MESH
        )

    def exchange(source, target, send, recv, rows):
        copies = []
        for peer in peers:
            copy = remote(
                source.at[piece(peer, rows), :], target.at[piece(rank, rows), :], send.at[peer], recv.at[rank],
                {"space": base + peer},
            )
            copy.start()
            copies.append(copy)
        target[piece(rank, rows), :] = source[piece(rank, rows), :]
        return copies

    def await_piece(peer, source, target, send, recv, rows):
        remote(
            source.at[piece(rank, rows), :], target.at[piece(peer, rows), :], send.at[peer], recv.at[peer],
            {"space": base + peer},
        ).wait_recv()

    def exchange_half(half, source, target, send, recv, spot):
        copies = []
        for peer in peers:
            copy = remote(
                source.at[spot(half, peer), :], target.at[place(half, rank), :], send.at[half, peer],
                recv.at[half, rank], {"space": base + peer},
            )
            copy.start()
            copies.append(copy)
        target[place(half, rank), :] = source[spot(half, rank), :]
        return copies

    def await_half(half, peer, source, target, send, recv, spot):
        remote(
            source.at[spot(half, rank), :], target.at[place(half, peer), :], send.at[half, peer],
            recv.at[half, peer], {"space": base + peer},
        ).wait_recv()

    def place(half, rank_index):
        return pl.ds(pl.multiple_of(rank_index * ROWS + half * HALF, HALF), HALF)

    def solved(half, rank_index):
        return pl.ds(pl.multiple_of(half * RANKS * HALF + rank_index * HALF, HALF), HALF)

    def solved_rows(half, owner):
        return pl.ds(half * RANKS * HALF + owner * HALF, HALF)

    def friction(low_row=0, high_row=ROWS):
        for start in range(low_row, high_row, 4):
            cols = pl.ds(start * LANES, 4 * LANES)
            both = jnp.dot(ahead[...], mix[0:32, cols], preferred_element_type=jnp.float32)
            velocity = both[:SAMPLES] + both[SAMPLES:]
            for q in range(4):
                r = start + q
                part = velocity[:, q * LANES:(q + 1) * LANES]
                stress = jnp.broadcast_to(drag[pl.ds(r, 1), :], part.shape) * jnp.abs(part) * part
                high, low = split(stress)
                mix[32:80, pl.ds(r * LANES, LANES)] = high
                mix[80:128, pl.ds(r * LANES, LANES)] = low
            both = jnp.dot(back[...], mix[:, cols], preferred_element_type=jnp.float32)
            back_terms[:, cols] = both[:COMPS] + both[COMPS:]

    def local_terms(it, low_row, high_row):
        for r in range(low_row, high_row):
            value = cur[it, comps(r), :]
            left = jnp.where(lane == 0, 0.0, shift(value, 1))
            right = jnp.where(lane == LANES - 1, 0.0, shift(value, LANES - 1))
            neighbours = left + right
            if r > 0:
                neighbours = neighbours + cur[it, comps(r - 1), :]
            if r < high_row - 1:
                neighbours = neighbours + cur[it, comps(r + 1), :]
            total = value + back_terms[:, pl.ds(r * LANES, LANES)] + spread(stiff, r) * (4.0 * value - neighbours)
            terms[comps(r), :] = total

    def local_residual(it, low_row, high_row):
        count = high_row - low_row
        for c in range(COMPS):
            rows = pl.ds(c * ROWS + low_row, count)
            fallen = terms[pl.ds(low_row * COMPS + c, count, stride=COMPS), :]
            fwd_out[it, rows, :] = wet[low_row:high_row] * (forcing[rows, :] - fallen)

    def lane_column(row):
        return jnp.sum(jnp.where(block_lane == block_row, jnp.broadcast_to(row, block), 0.0), axis=1, keepdims=True)

    def edge_terms(owner, it):
        value = fwd_in[it, piece(owner), :]
        north_row = jnp.broadcast_to(fix[pl.ds(owner + 2 * RANKS, 1), :], block)
        south_row = jnp.broadcast_to(fix[pl.ds(owner + 3 * RANKS, 1), :], block)
        value = value + jnp.where(block_row == 0, north_row, 0.0) + jnp.where(block_row == ROWS - 1, south_row, 0.0)
        if it == 1:
            west_col = lane_column(fix[pl.ds(owner, 1), :])
            east_col = lane_column(fix[pl.ds(owner + RANKS, 1), :])
            value = value + jnp.where(block_lane == 0, west_col, 0.0)
            value = value + jnp.where(block_lane == LANES - 1, east_col, 0.0)
            mid_row = jnp.broadcast_to(mid[pl.ds(owner, 1), :], block)
            value = value + jnp.where(block_row == HALF - 1, mid_row, 0.0)
        high, low = split(value)
        zonal_lhs[piece(owner), 0:LANES] = high
        zonal_lhs[piece(owner), LANES:2 * LANES] = low

    def meridional(rows, high, pair):
        both = jnp.dot(mer_high[rows, :], pair, preferred_element_type=jnp.float32)
        third = jnp.dot(mer_low[rows, :], high, preferred_element_type=jnp.float32)
        return both[:, :LANES] + both[:, LANES:] + third

    def device_rows(value, owner):
        first_half = value[owner * HALF:(owner + 1) * HALF]
        second_half = value[(RANKS + owner) * HALF:(RANKS + owner + 1) * HALF]
        return jnp.concatenate([first_half, second_half], axis=0)

    def solve(it):
        both = jnp.dot(zonal_lhs[...], zonal_w[...], preferred_element_type=jnp.float32)
        high, low = split(both[:, :LANES] + both[:, LANES:])
        pair = jnp.concatenate([high, low], axis=1)
        copies = []
        for half in range(2):
            rows = pl.ds(half * RANKS * HALF, RANKS * HALF)
            ret_out[it, rows, :] = meridional(rows, high, pair)
            copies.extend(exchange_half(half, *returns(it)))
        return copies

    def returns(it):
        return ret_out.at[it], ret_in.at[it], ret_send.at[it], ret_recv.at[it], solved

    pending = []
    loads[2].wait()
    first = jnp.zeros(tile, jnp.float32)
    last = jnp.zeros(tile, jnp.float32)
    for r in range(ROWS):
        value = spread(wet, r) * tide[pl.ds(r, COMPS, stride=ROWS), :]
        set_state(0, r, value)
        first = jnp.where(lane == r, shift(value, r), first)
        last = jnp.where(lane == r, shift(value, r + 1), last)
    wets = wet[...]
    strength = wets * stiff[...]
    packed = jnp.sum(
        columns_to_lanes(wets[:, 0:1], 0)
        + columns_to_lanes(wets[:, LANES - 1:LANES], 32)
        + columns_to_lanes(strength[:, 0:1], 64)
        + columns_to_lanes(strength[:, LANES - 1:LANES], 96),
        axis=0,
        keepdims=True,
    )
    for slot, value, extra in (
        (0, cur[0, comps(ROWS - 1), :], wets[ROWS - 1:ROWS]),
        (1, cur[0, comps(0), :], wets[0:1]),
        (2, last, shift(packed, LANES - 32)),
        (3, first, packed),
    ):
        halo_out[slot, 0:COMPS, :] = value
        halo_out[slot, COMPS:COMPS + 8, :] = jnp.broadcast_to(extra, (8, LANES))
    friction()
    pl.semaphore_wait(barrier, 5 + len(peers))
    halos = []
    for slot, device in ((2, east), (3, west), (0, south), (1, north)):
        copy = remote(halo_out.at[slot], halo_in.at[slot], halo_send.at[slot], halo_recv.at[slot], device)
        copy.start()
        halos.append(copy)
    pending.extend(halos)
    local_terms(0, 0, ROWS)
    loads[3].wait()
    local_residual(0, 0, ROWS)
    fwd = (fwd_out.at[0], fwd_in.at[0], fwd_send.at[0, 0], fwd_recv.at[0, 0], ROWS)
    pending.extend(exchange(*fwd))

    halo_of = {2: halos[0], 3: halos[1], 0: halos[2], 1: halos[3]}
    edges = ((0, strength[0:1], rank == 0), (1, strength[ROWS - 1:ROWS], rank == RANKS - 1))

    def edge_row(slot, factor):
        return jnp.broadcast_to(factor, tile) * halo_in[slot, 0:COMPS, :]

    def edge_factor(slot, factor):
        return 0.25 * jnp.broadcast_to(factor * halo_in[slot, COMPS:COMPS + 1, :], tile)

    for slot, factor, is_far in edges:
        @pl.when(is_far)
        def _():
            rim_out[pl.ds(slot, COMPS, stride=8), :] = jnp.zeros(tile, jnp.float32)

        @pl.when(jnp.logical_not(is_far))
        def _():
            halo_of[slot].wait_recv()
            rim_out[pl.ds(slot, COMPS, stride=8), :] = edge_row(slot, factor)

    factors = jnp.broadcast_to(strength[HALF - 1:HALF], tile)
    rim_out[pl.ds(2, COMPS, stride=8), :] = factors * cur[0, comps(HALF), :]
    rim_out[pl.ds(3, COMPS, stride=8), :] = 0.25 * factors * jnp.broadcast_to(wets[HALF:HALF + 1], tile)
    for j in range(4, 8):
        rim_out[pl.ds(j, COMPS, stride=8), :] = jnp.zeros(tile, jnp.float32)
    rims = (rim_out, rim_in, rim_send, rim_recv, 8)
    pending.extend(exchange(*rims))

    far[...] = jnp.zeros(tile, jnp.float32)
    for slot, factor, is_far in edges:
        @pl.when(is_far)
        def _():
            halo_of[slot].wait_recv()
            far[...] = edge_row(slot, factor * (has_north if slot == 0 else has_south))

    halo_of[2].wait_recv()
    halo_of[3].wait_recv()
    west_factor, east_factor = shift(packed, 64), shift(packed, 32)
    for j, value in enumerate((
        edge_row(2, west_factor),
        edge_row(3, east_factor),
        far[...],
        edge_factor(2, west_factor),
        edge_factor(3, east_factor),
        edge_factor(0, strength[0:1] * has_north),
        edge_factor(1, strength[ROWS - 1:ROWS] * has_south),
        jnp.zeros(tile, jnp.float32),
    )):
        fix_out[pl.ds(j, COMPS, stride=8), :] = value
    fixes = (fix_out, fix_in, fix_send, fix_recv, 8)
    pending.extend(exchange(*fixes))

    loads[4].wait()
    loads[5].wait()
    high, low = split(jnp.transpose(zonal_raw[owned]))
    zonal_w[0:128, 0:128] = high
    zonal_w[0:128, 128:256] = low
    zonal_w[128:256, 0:128] = high
    zonal_w[128:256, 128:256] = jnp.zeros((LANES, LANES), jnp.bfloat16)
    for owner in range(RANKS):
        for half in range(2):
            start = owner * ROWS + half * HALF
            high, low = split(mer_raw[start:start + HALF, :])
            mer_high[solved_rows(half, owner), :] = high
            mer_low[solved_rows(half, owner), :] = low

    square = (LANES, LANES)
    diagonal = iota(square, 0) == iota(square, 1)
    for k in range(COMPS // 2):
        for column, shape_ref in ((0, shape_w), (LANES - 1, shape_e)):
            values = jnp.broadcast_to(zonal_raw[k][:, column:column + 1], square)
            row = jnp.sum(jnp.where(diagonal, values, 0.0), axis=0, keepdims=True)
            shape_ref[2 * k:2 * k + 2, :] = jnp.broadcast_to(row, (2, LANES))

    for peer in peers:
        await_piece(peer, *fwd)
    for peer in peers:
        await_piece(peer, *rims)
    for j in range(2):
        fix[(2 + j) * RANKS:(3 + j) * RANKS, :] = rim_in[pl.ds(j, RANKS, stride=8), :]
    for owner in range(RANKS):
        edge_terms(owner, 0)
    pending.extend(solve(0))

    for peer in peers:
        await_piece(peer, *fixes)
    lower = (space >= RANKS).astype(jnp.float32)
    upper = 1.0 - lower
    for owner in range(RANKS):
        west_col = lane_column(fix_in[owner * 8:owner * 8 + 1, :])
        east_col = lane_column(fix_in[owner * 8 + 1:owner * 8 + 2, :])
        value = jnp.where(block_lane == 0, west_col, 0.0) + jnp.where(block_lane == 1, east_col, 0.0)
        if owner == 0:
            value = value + jnp.where((block_lane == 2) & (block_row == 0), lower, 0.0)
        if owner == RANKS - 1:
            value = value + jnp.where((block_lane == 2) & (block_row == ROWS - 1), upper, 0.0)
        high, low = split(value)
        zonal_lhs[piece(owner), 0:LANES] = high
        zonal_lhs[piece(owner), LANES:2 * LANES] = low
    heights = meridional(pl.ds(0, LM), zonal_lhs[:, 0:LANES], zonal_lhs[...])
    crossing = fix_in[2:3, :] + fix_in[(RANKS - 1) * 8 + 2:(RANKS - 1) * 8 + 3, :]
    high, low = split(jnp.broadcast_to(crossing, tile))
    both = jnp.dot(jnp.concatenate([high, low], axis=1), zonal_w[...], preferred_element_type=jnp.float32)
    crossing = (both[:, :LANES] + both[:, LANES:])[0:1]
    for owner in range(RANKS):
        value = device_rows(heights, owner)
        along = jnp.sum(
            columns_to_lanes(value[:, 0:1], 0)
            + columns_to_lanes(value[:, 1:2], 32)
            + columns_to_lanes(value[:, 2:3], 64),
            axis=0,
            keepdims=True,
        )
        late_out[owner * 8:owner * 8 + 1, :] = along
        late_out[owner * 8 + 1:owner * 8 + 8, :] = jnp.broadcast_to(crossing, (7, LANES))
    lates = (late_out, late_in, late_send, late_recv, 8)
    pending.extend(exchange(*lates))

    mine = pl.ds(rank, 1)
    flat = (LM, LANES)
    full[...] = (
        ret_out[0]
        + jnp.broadcast_to(heights[:, 0:1], flat) * jnp.broadcast_to(shape_w[mine, :], flat)
        + jnp.broadcast_to(heights[:, 1:2], flat) * jnp.broadcast_to(shape_e[mine, :], flat)
        + jnp.broadcast_to(heights[:, 2:3], flat) * jnp.broadcast_to(crossing, flat)
    )
    for owner in range(RANKS):
        value = jnp.concatenate([full[solved_rows(0, owner), :], full[solved_rows(1, owner), :]], axis=0)
        end_out[owner:owner + 1, :] = jnp.sum(
            columns_to_lanes(value[:, 0:1], 0) + columns_to_lanes(value[:, LANES - 1:LANES], 32), axis=0, keepdims=True
        )
    end_out[16:17, :] = full[0:1, :]
    end_out[17:24, :] = jnp.broadcast_to(full[LM - 1:LM, :], (7, LANES))
    ends = []
    for slot, device in ((0, east), (1, west), (2, across)):
        copy = remote(end_out, end_in.at[slot], end_send.at[slot], end_recv.at[slot], device)
        copy.start()
        ends.append(copy)
    pending.extend(ends)

    for half in range(2):
        for peer in peers:
            await_half(half, peer, *returns(0))
        if half == 0:
            for peer in peers:
                await_piece(peer, *lates)
            along = late_in[pl.ds(0, COMPS, stride=8), :]
            shapes = (shape_w[...], shape_e[...], late_in[pl.ds(1, COMPS, stride=8), :])
        low_row, high_row = half * HALF, (half + 1) * HALF
        for r in range(low_row, high_row):
            step = ret_in[0, pl.ds(r, COMPS, stride=ROWS), :]
            for j, shape in enumerate(shapes):
                step = step + jnp.broadcast_to(along[:, ROWS * j + r:ROWS * j + r + 1], tile) * shape
            set_state(1, r, cur[0, comps(r), :] + 0.25 * spread(wet, r) * step)
        friction(low_row, high_row)
        local_terms(1, low_row, high_row)
        local_residual(1, low_row, high_row)
        pending.extend(exchange_half(half, fwd_out.at[1], fwd_in.at[1], fwd_send.at[1], fwd_recv.at[1], place))

    for copy in ends:
        copy.wait_recv()
    norths = jnp.concatenate(
        [end_in[2, 17:18, :], full[pl.ds(RANKS * HALF + HALF - 1, RANKS, stride=HALF), :][:RANKS - 1]], axis=0
    )
    souths = jnp.concatenate([full[pl.ds(0, RANKS, stride=HALF), :][1:], end_in[2, 16:17, :]], axis=0)
    crossed = fix_in[pl.ds(2, RANKS, stride=8), :]
    bases = (
        fix_in[pl.ds(0, RANKS, stride=8), :],
        fix_in[pl.ds(1, RANKS, stride=8), :],
        rim_in[pl.ds(0, RANKS, stride=8), :] + lower * crossed,
        rim_in[pl.ds(1, RANKS, stride=8), :] + upper * crossed,
    )
    steps = (shift(end_in[0, 0:RANKS, :], LANES - 32), end_in[1, 0:RANKS, :], norths, souths)
    for j in range(4):
        fix[j * RANKS:(j + 1) * RANKS, :] = bases[j] + fix_in[pl.ds(3 + j, RANKS, stride=8), :] * steps[j]
    mid[...] = rim_in[pl.ds(2, RANKS, stride=8), :] + rim_in[pl.ds(3, RANKS, stride=8), :] * full[
        pl.ds(RANKS * HALF, RANKS, stride=HALF), :
    ]
    edge_terms(rank, 1)
    for peer in peers[::-1]:
        for half in range(2):
            await_half(half, peer, fwd_out.at[1], fwd_in.at[1], fwd_send.at[1], fwd_recv.at[1], place)
        edge_terms(peer, 1)
    pending.extend(solve(1))
    for half in range(2):
        for peer in peers:
            await_half(half, peer, *returns(1))
        for c in range(COMPS):
            rows = pl.ds(c * ROWS + half * HALF, HALF)
            state = cur[1, pl.ds(half * HALF * COMPS + c, HALF, stride=COMPS), :]
            out_ref[rows, :] = state + 0.25 * wet[half * HALF:(half + 1) * HALF] * ret_in[1, rows, :]
    for copy in pending:
        copy.wait_send()


def body(
    tide_state,
    forcing,
    wet_mask,
    depth_band,
    drag_table,
    stiff_table,
    sample_times,
    zonal_inverse,
    meridional_inverse,
):
    flat = (COMPS * ROWS, LANES)
    f32, bf16 = jnp.float32, jnp.bfloat16
    dma = pltpu.SemaphoreType.DMA
    any_spec = pl.BlockSpec(memory_space=pltpu.HBM)
    smem = pl.BlockSpec(memory_space=pltpu.SMEM)
    result = pl.pallas_call(
        kernel,
        out_shape=pltpu.VMEM(flat, f32),
        in_specs=[any_spec] * 4 + [smem] * 3 + [any_spec] * 2,
        out_specs=pl.BlockSpec(memory_space=pltpu.VMEM),
        scratch_shapes=[
            pltpu.VMEM(flat, f32),
            pltpu.VMEM(flat, f32),
            pltpu.VMEM((ROWS, LANES), jnp.int32),
            pltpu.VMEM((ROWS, LANES), jnp.int32),
            pltpu.VMEM((COMPS // 2, LANES, LANES), f32),
            pltpu.VMEM((LM, LM), f32),
            pltpu.VMEM((ROWS, LANES), f32),
            pltpu.VMEM((ROWS, LANES), f32),
            pltpu.VMEM((ROWS, LANES), f32),
            pltpu.VMEM((96, 32), bf16),
            pltpu.VMEM((32, LANES), bf16),
            pltpu.VMEM((256, 256), bf16),
            pltpu.VMEM((LM, LM), bf16),
            pltpu.VMEM((LM, LM), bf16),
            pltpu.VMEM((ITERS,) + flat, f32),
            pltpu.VMEM((LANES, ROWS * LANES), bf16),
            pltpu.VMEM((COMPS, ROWS * LANES), f32),
            pltpu.VMEM(flat, f32),
            pltpu.VMEM((4, COMPS + 8, LANES), f32),
            pltpu.VMEM((4, COMPS + 8, LANES), f32),
            pltpu.VMEM((8 * RANKS, LANES), f32),
            pltpu.VMEM((8 * RANKS, LANES), f32),
            pltpu.VMEM((4 * RANKS, LANES), f32),
            pltpu.VMEM((RANKS + 8, LANES), f32),
            pltpu.VMEM((3, RANKS + 8, LANES), f32),
            pltpu.VMEM((8 * RANKS, LANES), f32),
            pltpu.VMEM((8 * RANKS, LANES), f32),
            pltpu.VMEM((COMPS, LANES), f32),
            pltpu.VMEM((8 * RANKS, LANES), f32),
            pltpu.VMEM((8 * RANKS, LANES), f32),
            pltpu.VMEM(flat, f32),
            pltpu.VMEM((COMPS, LANES), f32),
            pltpu.VMEM((COMPS, LANES), f32),
            pltpu.VMEM((RANKS, LANES), f32),
            pltpu.VMEM((LM, 2 * LANES), bf16),
            pltpu.VMEM((ITERS,) + flat, f32),
            pltpu.VMEM((ITERS,) + flat, f32),
            pltpu.VMEM((ITERS,) + flat, f32),
            pltpu.VMEM((ITERS,) + flat, f32),
            dma((6,)),
            dma((4,)),
            dma((4,)),
            dma((RANKS,)),
            dma((RANKS,)),
            dma((3,)),
            dma((3,)),
            dma((RANKS,)),
            dma((RANKS,)),
            dma((RANKS,)),
            dma((RANKS,)),
            dma((ITERS, 2, RANKS)),
            dma((ITERS, 2, RANKS)),
            dma((ITERS, 2, RANKS)),
            dma((ITERS, 2, RANKS)),
        ],
        compiler_params=pltpu.CompilerParams(
            collective_id=0, has_side_effects=True, vmem_limit_bytes=60 * 1024 * 1024
        ),
        cost_estimate=pl.CostEstimate(flops=600000000, bytes_accessed=2500000, transcendentals=0),
    )(
        tide_state.reshape(flat),
        forcing.reshape(flat),
        wet_mask,
        depth_band,
        drag_table,
        stiff_table,
        sample_times,
        zonal_inverse,
        meridional_inverse,
    )
    return result.reshape(tide_state.shape)


def solution(mesh):
    grid = P(None, None, "space", "samp")
    return jax.shard_map(
        body,
        mesh=mesh,
        in_specs=(grid, grid, P("space", "samp"), P("space", "samp"), P(), P(), P(), P(), P()),
        out_specs=grid,
        check_vma=False,
    )
```

```python
import functools

import jax
import jax.numpy as jnp
from jax import lax
from jax.experimental import pallas as pl
from jax.experimental.pallas import tpu as pltpu
from jax.sharding import PartitionSpec as P

MESH = pl.DeviceIdType.MESH
ITERS = 2
ROWS = 32
HALF = 16
LANES = 128
COMPS = 16
SAMPLES = 48
RANKS = 16
CHIPS = 8
LM = 512

TIDAL_FREQUENCIES = (
    0.505868,
    0.5235988,
    0.4963657,
    0.5250316,
    0.2625162,
    0.2433523,
    0.2610812,
    0.2338335,
)

OFFSETS = [(dy, dc) for dy in (4, 3, 5, 2, 6, 1, 7) for dc in (0, 1)] + [(0, 1)]


def rotated_cosine(phase, quarter):
    turns = jnp.floor(phase * 0.63661977236758134308 + 0.5)
    rest = phase - turns * 1.5703125
    rest = rest - turns * 4.837512969970703125e-4
    rest = rest - turns * 7.54978995489188216e-8
    quadrant = (turns.astype(jnp.int32) + quarter) & 3
    square = rest * rest
    cosine = 1.0 + square * (
        -0.5 + square * (4.166664568298827e-2 + square * (-1.388731625493765e-3 + square * 2.443315711809948e-5))
    )
    sine = rest + rest * square * (
        -1.6666654611e-1 + square * (8.3321608736e-3 + square * -1.9515295891e-4)
    )
    value = jnp.where((quadrant & 1) == 1, -sine, cosine)
    return jnp.where(quadrant >= 2, -value, value)


def speeds_at(component):
    constituent = component >> 1
    speeds = jnp.zeros(component.shape, jnp.float32)
    for index, speed in enumerate(TIDAL_FREQUENCIES):
        speeds = jnp.where(constituent == index, jnp.float32(speed), speeds)
    return speeds


def high_part(value):
    return value.astype(jnp.bfloat16).astype(jnp.float32)


def split(value):
    high = value.astype(jnp.bfloat16)
    low = (value - high.astype(jnp.float32)).astype(jnp.bfloat16)
    return high, low


def iota(shape, dim):
    return lax.broadcasted_iota(jnp.int32, shape, dim)


def build_factors(times_ref, ahead_ref, back_ref):
    lane = iota((8, LANES), 1)
    row_times = jnp.zeros((8, LANES), jnp.float32)
    ahead_times = jnp.zeros((8, LANES), jnp.float32)
    for t in range(SAMPLES):
        value = times_ref[t]
        row_times = jnp.where((lane == 32 + t) | (lane == 80 + t), value, row_times)
        ahead_times = jnp.where((lane == t) | (lane == 48 + t), value, ahead_times)
    column_times = jnp.transpose(jnp.broadcast_to(ahead_times[0:1], (LANES, LANES)))[:96, :32]
    shape = (96, 32)
    col = iota(shape, 1)
    comp = col & 15
    value = rotated_cosine(column_times * speeds_at(comp), comp & 1)
    high = high_part(value)
    low = jnp.where(col < 16, value - high, 0.0)
    ahead_ref[...] = jnp.where(iota(shape, 0) < 48, high, low).astype(jnp.bfloat16)
    shape = (32, LANES)
    row, col = iota(shape, 0), iota(shape, 1)
    comp = row & 15
    speed = speeds_at(comp)
    times = jnp.broadcast_to(row_times[0:1], shape)
    basis = rotated_cosine(times * speed, comp & 1)
    other = col & 15
    turn = jnp.where(other == (comp ^ 1), jnp.where((comp & 1) == 0, -speed, speed), 0.0)
    value = jnp.where(col < 32, turn, basis)
    high = high_part(value)
    low_used = (col < 16) | ((col >= 32) & (col < 80))
    low = jnp.where(low_used, value - high, 0.0)
    back_ref[...] = jnp.where(row < 16, high, low).astype(jnp.bfloat16)


def kernel(
    tide_hbm, forcing_hbm, wet_hbm, band_hbm, drag_ref, stiff_ref, times_ref, zonal_hbm, meridional_hbm,
    out_ref,
    tide, forcing, wet_int, band, zonal_raw, mer_raw,
    wet, drag, stiff, ahead, back, zonal_w, mer_high, mer_low,
    cur, mix, back_terms, terms, halo_out, halo_in, fix_out, fix_in, fix, end_out, end_in, mid_out, mid_in, mid, zonal_lhs,
    fwd_out, fwd_in, ret_out, ret_in,
    local_sem, halo_send, halo_recv, fix_send, fix_recv, end_send, end_recv, mid_send, mid_recv, fwd_send, fwd_recv, ret_send, ret_recv,
):
    samp = lax.axis_index("samp")
    space = lax.axis_index("space")
    n_samp = lax.axis_size("samp")
    n_space = lax.axis_size("space")
    rank = space % RANKS
    base = space - rank
    chip, core = rank // 2, rank % 2
    owned = rank // 2

    loads = [
        pltpu.make_async_copy(wet_hbm, wet_int, local_sem.at[0]),
        pltpu.make_async_copy(band_hbm, band, local_sem.at[1]),
        pltpu.make_async_copy(tide_hbm, tide, local_sem.at[2]),
        pltpu.make_async_copy(forcing_hbm, forcing, local_sem.at[3]),
        pltpu.make_async_copy(zonal_hbm.at[owned], zonal_raw, local_sem.at[4]),
        pltpu.make_async_copy(meridional_hbm.at[owned], mer_raw, local_sem.at[5]),
    ]
    for load in loads:
        load.start()

    north = {"space": (space + n_space - 1) % n_space}
    south = {"space": (space + 1) % n_space}
    west = {"samp": (samp + n_samp - 1) % n_samp}
    east = {"samp": (samp + 1) % n_samp}
    across = {"space": (space + RANKS) % n_space}

    peers = []
    for dy, dc in OFFSETS:
        peers.append(((chip + dy) % CHIPS) * 2 + (core + dc) % 2)

    barrier = pltpu.get_barrier_semaphore()
    for target in [north, south, west, east, across] + [{"space": base + peer} for peer in peers]:
        pl.semaphore_signal(barrier, inc=1, device_id=target, device_id_type=MESH)

    loads[0].wait()
    wet[...] = wet_int[...].astype(jnp.float32)
    tile = (COMPS, LANES)
    lane = iota(tile, 1)
    block = (ROWS, LANES)
    block_row, block_lane = iota(block, 0), iota(block, 1)
    has_north = (space > 0).astype(jnp.float32)
    has_south = (space < n_space - 1).astype(jnp.float32)

    def shift(value, amount):
        amount = amount % LANES
        return value if amount == 0 else pltpu.roll(value, amount, 1)

    def comps(r):
        return pl.ds(r * COMPS, COMPS)

    def spread(ref, r):
        return jnp.broadcast_to(ref[pl.ds(r, 1), :], tile)

    def piece(rank_index, rows=ROWS):
        return pl.ds(pl.multiple_of(rank_index * rows, rows), rows)

    def columns_to_lanes(value, first_lane):
        picked = jnp.where(block_lane == block_row + first_lane, jnp.broadcast_to(value, block), 0.0)
        return picked

    def set_state(it, r, value):
        cur[it, comps(r), :] = value
        high, low = split(value)
        cols = pl.ds(r * LANES, LANES)
        mix[0:16, cols] = high
        mix[16:32, cols] = low

    def remote(source, target, send, recv, device):
        return pltpu.make_async_remote_copy(
            src_ref=source, dst_ref=target, send_sem=send, recv_sem=recv, device_id=device, device_id_type=MESH
        )

    def exchange(source, target, send, recv, rows):
        copies = []
        for peer in peers:
            copy = remote(
                source.at[piece(peer, rows), :], target.at[piece(rank, rows), :], send.at[peer], recv.at[rank],
                {"space": base + peer},
            )
            copy.start()
            copies.append(copy)
        target[piece(rank, rows), :] = source[piece(rank, rows), :]
        return copies

    def await_piece(peer, source, target, send, recv, rows):
        remote(
            source.at[piece(rank, rows), :], target.at[piece(peer, rows), :], send.at[peer], recv.at[peer],
            {"space": base + peer},
        ).wait_recv()

    def exchange_half(half, source, target, send, recv, spot):
        copies = []
        for peer in peers:
            copy = remote(
                source.at[spot(half, peer), :], target.at[place(half, rank), :], send.at[half, peer],
                recv.at[half, rank], {"space": base + peer},
            )
            copy.start()
            copies.append(copy)
        target[place(half, rank), :] = source[spot(half, rank), :]
        return copies

    def await_half(half, peer, source, target, send, recv, spot):
        remote(
            source.at[spot(half, rank), :], target.at[place(half, peer), :], send.at[half, peer],
            recv.at[half, peer], {"space": base + peer},
        ).wait_recv()

    def place(half, rank_index):
        return pl.ds(pl.multiple_of(rank_index * ROWS + half * HALF, HALF), HALF)

    def solved(half, rank_index):
        return pl.ds(pl.multiple_of(half * RANKS * HALF + rank_index * HALF, HALF), HALF)

    def solved_rows(half, owner):
        return pl.ds(half * RANKS * HALF + owner * HALF, HALF)

    def friction(low_row=0, high_row=ROWS):
        for start in range(low_row, high_row, 4):
            cols = pl.ds(start * LANES, 4 * LANES)
            both = jnp.dot(ahead[...], mix[0:32, cols], preferred_element_type=jnp.float32)
            velocity = both[:SAMPLES] + both[SAMPLES:]
            for q in range(4):
                r = start + q
                part = velocity[:, q * LANES:(q + 1) * LANES]
                stress = jnp.broadcast_to(drag[pl.ds(r, 1), :], part.shape) * jnp.abs(part) * part
                high, low = split(stress)
                mix[32:80, pl.ds(r * LANES, LANES)] = high
                mix[80:128, pl.ds(r * LANES, LANES)] = low
            both = jnp.dot(back[...], mix[:, cols], preferred_element_type=jnp.float32)
            back_terms[:, cols] = both[:COMPS] + both[COMPS:]

    def local_terms(it, low_row, high_row):
        for r in range(low_row, high_row):
            value = cur[it, comps(r), :]
            left = jnp.where(lane == 0, 0.0, shift(value, 1))
            right = jnp.where(lane == LANES - 1, 0.0, shift(value, LANES - 1))
            neighbours = left + right
            if r > 0:
                neighbours = neighbours + cur[it, comps(r - 1), :]
            if r < high_row - 1:
                neighbours = neighbours + cur[it, comps(r + 1), :]
            total = value + back_terms[:, pl.ds(r * LANES, LANES)] + spread(stiff, r) * (4.0 * value - neighbours)
            terms[comps(r), :] = total

    def local_residual(it, low_row, high_row):
        count = high_row - low_row
        for c in range(COMPS):
            rows = pl.ds(c * ROWS + low_row, count)
            fallen = terms[pl.ds(low_row * COMPS + c, count, stride=COMPS), :]
            fwd_out[it, rows, :] = wet[low_row:high_row] * (forcing[rows, :] - fallen)

    def edge_terms(owner, it):
        value = fwd_in[it, piece(owner), :]
        west_row = jnp.broadcast_to(fix[pl.ds(owner, 1), :], block)
        east_row = jnp.broadcast_to(fix[pl.ds(owner + RANKS, 1), :], block)
        north_row = jnp.broadcast_to(fix[pl.ds(owner + 2 * RANKS, 1), :], block)
        south_row = jnp.broadcast_to(fix[pl.ds(owner + 3 * RANKS, 1), :], block)
        same = block_lane == block_row
        west_col = jnp.sum(jnp.where(same, west_row, 0.0), axis=1, keepdims=True)
        east_col = jnp.sum(jnp.where(same, east_row, 0.0), axis=1, keepdims=True)
        value = value + jnp.where(block_lane == 0, west_col, 0.0) + jnp.where(block_lane == LANES - 1, east_col, 0.0)
        value = value + jnp.where(block_row == 0, north_row, 0.0) + jnp.where(block_row == ROWS - 1, south_row, 0.0)
        if it == 1:
            mid_row = jnp.broadcast_to(mid[pl.ds(owner, 1), :], block)
            value = value + jnp.where(block_row == HALF - 1, mid_row, 0.0)
        high, low = split(value)
        zonal_lhs[piece(owner), 0:LANES] = high
        zonal_lhs[piece(owner), LANES:2 * LANES] = low

    def solve(it):
        both = jnp.dot(zonal_lhs[...], zonal_w[...], preferred_element_type=jnp.float32)
        high, low = split(both[:, :LANES] + both[:, LANES:])
        pair = jnp.concatenate([high, low], axis=1)
        copies = []
        for half in range(2):
            rows = pl.ds(half * RANKS * HALF, RANKS * HALF)
            both = jnp.dot(mer_high[rows, :], pair, preferred_element_type=jnp.float32)
            third = jnp.dot(mer_low[rows, :], high, preferred_element_type=jnp.float32)
            ret_out[it, rows, :] = both[:, :LANES] + both[:, LANES:] + third
            copies.extend(exchange_half(half, *returns(it)))
        return copies

    def returns(it):
        return ret_out.at[it], ret_in.at[it], ret_send.at[it], ret_recv.at[it], solved

    pending = []
    loads[2].wait()
    first = jnp.zeros(tile, jnp.float32)
    last = jnp.zeros(tile, jnp.float32)
    for r in range(ROWS):
        value = spread(wet, r) * tide[pl.ds(r, COMPS, stride=ROWS), :]
        set_state(0, r, value)
        first = jnp.where(lane == r, shift(value, r), first)
        last = jnp.where(lane == r, shift(value, r + 1), last)
    wets = wet[...]
    near_wets = jnp.sum(
        columns_to_lanes(wets[:, 0:1], 0) + columns_to_lanes(wets[:, LANES - 1:LANES], 32), axis=0, keepdims=True
    )
    for slot, value, extra in (
        (0, cur[0, comps(ROWS - 1), :], wets[ROWS - 1:ROWS]),
        (1, cur[0, comps(0), :], wets[0:1]),
        (2, last, shift(near_wets, LANES - 32)),
        (3, first, near_wets),
    ):
        halo_out[slot, 0:COMPS, :] = value
        halo_out[slot, COMPS:COMPS + 8, :] = jnp.broadcast_to(extra, (8, LANES))
    pl.semaphore_wait(barrier, 5 + len(peers))
    halos = []
    for slot, device in ((2, east), (3, west), (0, south), (1, north)):
        copy = remote(halo_out.at[slot], halo_in.at[slot], halo_send.at[slot], halo_recv.at[slot], device)
        copy.start()
        halos.append(copy)
    pending.extend(halos)
    build_factors(times_ref, ahead, back)
    loads[1].wait()
    drags = jnp.zeros((ROWS, LANES), jnp.float32)
    stiffs = jnp.zeros((ROWS, LANES), jnp.float32)
    for level in range(drag_ref.shape[0]):
        here = band[...] == level
        drags = jnp.where(here, drag_ref[level], drags)
        stiffs = jnp.where(here, stiff_ref[level], stiffs)
    drag[...] = drags * (2.0 / SAMPLES)
    stiff[...] = stiffs
    strength = wets * stiff[...]
    packed = jnp.sum(
        columns_to_lanes(strength[:, 0:1], 64) + columns_to_lanes(strength[:, LANES - 1:LANES], 96), axis=0, keepdims=True
    )
    friction()
    local_terms(0, 0, ROWS)
    loads[3].wait()
    local_residual(0, 0, ROWS)
    fwd = (fwd_out.at[0], fwd_in.at[0], fwd_send.at[0, 0], fwd_recv.at[0, 0], ROWS)
    pending.extend(exchange(*fwd))

    for copy in halos:
        copy.wait_recv()
    sides = (
        (2, shift(packed, 64)),
        (3, shift(packed, 32)),
        (0, strength[0:1] * has_north),
        (1, strength[ROWS - 1:ROWS] * has_south),
    )
    for j, (slot, factor) in enumerate(sides):
        factors = jnp.broadcast_to(factor, tile)
        near = jnp.broadcast_to(halo_in[slot, COMPS:COMPS + 1, :], tile)
        fix_out[pl.ds(j, COMPS, stride=8), :] = factors * halo_in[slot, 0:COMPS, :]
        fix_out[pl.ds(4 + j, COMPS, stride=8), :] = 0.25 * factors * near
    fixes = (fix_out, fix_in, fix_send, fix_recv, 8)
    pending.extend(exchange(*fixes))
    factors = jnp.broadcast_to(strength[HALF - 1:HALF], tile)
    mid_out[pl.ds(0, COMPS, stride=8), :] = factors * cur[0, comps(HALF), :]
    mid_out[pl.ds(1, COMPS, stride=8), :] = 0.25 * factors * jnp.broadcast_to(wets[HALF:HALF + 1], tile)
    for j in range(2, 8):
        mid_out[pl.ds(j, COMPS, stride=8), :] = jnp.zeros(tile, jnp.float32)
    mids = (mid_out, mid_in, mid_send, mid_recv, 8)
    pending.extend(exchange(*mids))

    loads[4].wait()
    loads[5].wait()
    high, low = split(jnp.transpose(zonal_raw[...]))
    zonal_w[0:128, 0:128] = high
    zonal_w[0:128, 128:256] = low
    zonal_w[128:256, 0:128] = high
    zonal_w[128:256, 128:256] = jnp.zeros((LANES, LANES), jnp.bfloat16)
    for owner in range(RANKS):
        for half in range(2):
            start = owner * ROWS + half * HALF
            high, low = split(mer_raw[start:start + HALF, :])
            mer_high[solved_rows(half, owner), :] = high
            mer_low[solved_rows(half, owner), :] = low

    for peer in peers:
        await_piece(peer, *fwd)
    for peer in peers:
        await_piece(peer, *fixes)
    for j in range(4):
        fix[j * RANKS:(j + 1) * RANKS, :] = fix_in[pl.ds(j, RANKS, stride=8), :]
    for owner in range(RANKS):
        edge_terms(owner, 0)
    pending.extend(solve(0))

    for owner in range(RANKS):
        value = jnp.concatenate([ret_out[0, solved_rows(0, owner), :], ret_out[0, solved_rows(1, owner), :]], axis=0)
        end_out[owner:owner + 1, :] = jnp.sum(
            columns_to_lanes(value[:, 0:1], 0) + columns_to_lanes(value[:, LANES - 1:LANES], 32), axis=0, keepdims=True
        )
    end_out[16:17, :] = ret_out[0, 0:1, :]
    end_out[17:24, :] = jnp.broadcast_to(ret_out[0, LM - 1:LM, :], (7, LANES))
    ends = []
    for slot, device in ((0, east), (1, west), (2, across)):
        copy = remote(end_out, end_in.at[slot], end_send.at[slot], end_recv.at[slot], device)
        copy.start()
        ends.append(copy)
    pending.extend(ends)

    for half in range(2):
        for peer in peers:
            await_half(half, peer, *returns(0))
        low_row, high_row = half * HALF, (half + 1) * HALF
        for r in range(low_row, high_row):
            step = ret_in[0, pl.ds(r, COMPS, stride=ROWS), :]
            set_state(1, r, cur[0, comps(r), :] + 0.25 * spread(wet, r) * step)
        friction(low_row, high_row)
        local_terms(1, low_row, high_row)
        local_residual(1, low_row, high_row)
        pending.extend(exchange_half(half, fwd_out.at[1], fwd_in.at[1], fwd_send.at[1], fwd_recv.at[1], place))

    for peer in peers:
        await_piece(peer, *mids)
    for copy in ends:
        copy.wait_recv()
    norths = jnp.concatenate([end_in[2, 17:18, :], ret_out[0, pl.ds(RANKS * HALF + HALF - 1, RANKS, stride=HALF), :][:RANKS - 1]], axis=0)
    souths = jnp.concatenate([ret_out[0, pl.ds(0, RANKS, stride=HALF), :][1:], end_in[2, 16:17, :]], axis=0)
    steps = (shift(end_in[0, 0:RANKS, :], LANES - 32), end_in[1, 0:RANKS, :], norths, souths)
    for j, step in enumerate(steps):
        fix[j * RANKS:(j + 1) * RANKS, :] = (
            fix_in[pl.ds(j, RANKS, stride=8), :] + fix_in[pl.ds(4 + j, RANKS, stride=8), :] * step
        )
    mid[...] = mid_in[pl.ds(0, RANKS, stride=8), :] + mid_in[pl.ds(1, RANKS, stride=8), :] * ret_out[
        0, pl.ds(RANKS * HALF, RANKS, stride=HALF), :
    ]
    edge_terms(rank, 1)
    for peer in peers[::-1]:
        for half in range(2):
            await_half(half, peer, fwd_out.at[1], fwd_in.at[1], fwd_send.at[1], fwd_recv.at[1], place)
        edge_terms(peer, 1)
    pending.extend(solve(1))
    for half in range(2):
        for peer in peers:
            await_half(half, peer, *returns(1))
        for c in range(COMPS):
            rows = pl.ds(c * ROWS + half * HALF, HALF)
            state = cur[1, pl.ds(half * HALF * COMPS + c, HALF, stride=COMPS), :]
            out_ref[rows, :] = state + 0.25 * wet[half * HALF:(half + 1) * HALF] * ret_in[1, rows, :]
    for copy in pending:
        copy.wait_send()


def body(
    tide_state,
    forcing,
    wet_mask,
    depth_band,
    drag_table,
    stiff_table,
    sample_times,
    zonal_inverse,
    meridional_inverse,
):
    flat = (COMPS * ROWS, LANES)
    f32, bf16 = jnp.float32, jnp.bfloat16
    dma = pltpu.SemaphoreType.DMA
    any_spec = pl.BlockSpec(memory_space=pltpu.HBM)
    smem = pl.BlockSpec(memory_space=pltpu.SMEM)
    result = pl.pallas_call(
        kernel,
        out_shape=pltpu.VMEM(flat, f32),
        in_specs=[any_spec] * 4 + [smem] * 3 + [any_spec] * 2,
        out_specs=pl.BlockSpec(memory_space=pltpu.VMEM),
        scratch_shapes=[
            pltpu.VMEM(flat, f32),
            pltpu.VMEM(flat, f32),
            pltpu.VMEM((ROWS, LANES), jnp.int32),
            pltpu.VMEM((ROWS, LANES), jnp.int32),
            pltpu.VMEM((LANES, LANES), f32),
            pltpu.VMEM((LM, LM), f32),
            pltpu.VMEM((ROWS, LANES), f32),
            pltpu.VMEM((ROWS, LANES), f32),
            pltpu.VMEM((ROWS, LANES), f32),
            pltpu.VMEM((96, 32), bf16),
            pltpu.VMEM((32, LANES), bf16),
            pltpu.VMEM((256, 256), bf16),
            pltpu.VMEM((LM, LM), bf16),
            pltpu.VMEM((LM, LM), bf16),
            pltpu.VMEM((ITERS,) + flat, f32),
            pltpu.VMEM((LANES, ROWS * LANES), bf16),
            pltpu.VMEM((COMPS, ROWS * LANES), f32),
            pltpu.VMEM(flat, f32),
            pltpu.VMEM((4, COMPS + 8, LANES), f32),
            pltpu.VMEM((4, COMPS + 8, LANES), f32),
            pltpu.VMEM((8 * RANKS, LANES), f32),
            pltpu.VMEM((8 * RANKS, LANES), f32),
            pltpu.VMEM((4 * RANKS, LANES), f32),
            pltpu.VMEM((RANKS + 8, LANES), f32),
            pltpu.VMEM((3, RANKS + 8, LANES), f32),
            pltpu.VMEM((8 * RANKS, LANES), f32),
            pltpu.VMEM((8 * RANKS, LANES), f32),
            pltpu.VMEM((RANKS, LANES), f32),
            pltpu.VMEM((LM, 2 * LANES), bf16),
            pltpu.VMEM((ITERS,) + flat, f32),
            pltpu.VMEM((ITERS,) + flat, f32),
            pltpu.VMEM((ITERS,) + flat, f32),
            pltpu.VMEM((ITERS,) + flat, f32),
            dma((6,)),
            dma((4,)),
            dma((4,)),
            dma((RANKS,)),
            dma((RANKS,)),
            dma((3,)),
            dma((3,)),
            dma((RANKS,)),
            dma((RANKS,)),
            dma((ITERS, 2, RANKS)),
            dma((ITERS, 2, RANKS)),
            dma((ITERS, 2, RANKS)),
            dma((ITERS, 2, RANKS)),
        ],
        compiler_params=pltpu.CompilerParams(
            collective_id=0, has_side_effects=True, vmem_limit_bytes=60 * 1024 * 1024
        ),
        cost_estimate=pl.CostEstimate(flops=600000000, bytes_accessed=2500000, transcendentals=0),
    )(
        tide_state.reshape(flat),
        forcing.reshape(flat),
        wet_mask,
        depth_band,
        drag_table,
        stiff_table,
        sample_times,
        zonal_inverse,
        meridional_inverse,
    )
    return result.reshape(tide_state.shape)


def solution(mesh):
    grid = P(None, None, "space", "samp")
    return jax.shard_map(
        body,
        mesh=mesh,
        in_specs=(grid, grid, P("space", "samp"), P("space", "samp"), P(), P(), P(), P(), P()),
        out_specs=grid,
        check_vma=False,
    )
```

```python
import functools

import jax
import jax.numpy as jnp
from jax import lax
from jax.experimental import pallas as pl
from jax.experimental.pallas import tpu as pltpu
from jax.sharding import PartitionSpec as P

MESH = pl.DeviceIdType.MESH
ITERS = 2
ROWS = 32
HALF = 16
LANES = 128
COMPS = 16
SAMPLES = 48
RANKS = 16
CHIPS = 8
LM = 512

TIDAL_FREQUENCIES = (
    0.505868,
    0.5235988,
    0.4963657,
    0.5250316,
    0.2625162,
    0.2433523,
    0.2610812,
    0.2338335,
)

OFFSETS = [(dy, dc) for dy in (4, 3, 5, 2, 6, 1, 7) for dc in (0, 1)] + [(0, 1)]


def rotated_cosine(phase, quarter):
    turns = jnp.floor(phase * 0.63661977236758134308 + 0.5)
    rest = phase - turns * 1.5703125
    rest = rest - turns * 4.837512969970703125e-4
    rest = rest - turns * 7.54978995489188216e-8
    quadrant = (turns.astype(jnp.int32) + quarter) & 3
    square = rest * rest
    cosine = 1.0 + square * (
        -0.5 + square * (4.166664568298827e-2 + square * (-1.388731625493765e-3 + square * 2.443315711809948e-5))
    )
    sine = rest + rest * square * (
        -1.6666654611e-1 + square * (8.3321608736e-3 + square * -1.9515295891e-4)
    )
    value = jnp.where((quadrant & 1) == 1, -sine, cosine)
    return jnp.where(quadrant >= 2, -value, value)


def speeds_at(component):
    constituent = component >> 1
    speeds = jnp.zeros(component.shape, jnp.float32)
    for index, speed in enumerate(TIDAL_FREQUENCIES):
        speeds = jnp.where(constituent == index, jnp.float32(speed), speeds)
    return speeds


def high_part(value):
    return value.astype(jnp.bfloat16).astype(jnp.float32)


def split(value):
    high = value.astype(jnp.bfloat16)
    low = (value - high.astype(jnp.float32)).astype(jnp.bfloat16)
    return high, low


def iota(shape, dim):
    return lax.broadcasted_iota(jnp.int32, shape, dim)


def build_factors(times_ref, ahead_ref, back_ref):
    lane = iota((8, LANES), 1)
    row_times = jnp.zeros((8, LANES), jnp.float32)
    ahead_times = jnp.zeros((8, LANES), jnp.float32)
    for t in range(SAMPLES):
        value = times_ref[t]
        row_times = jnp.where((lane == 32 + t) | (lane == 80 + t), value, row_times)
        ahead_times = jnp.where((lane == t) | (lane == 48 + t), value, ahead_times)
    column_times = jnp.transpose(jnp.broadcast_to(ahead_times[0:1], (LANES, LANES)))[:96, :32]
    shape = (96, 32)
    col = iota(shape, 1)
    comp = col & 15
    value = rotated_cosine(column_times * speeds_at(comp), comp & 1)
    high = high_part(value)
    low = jnp.where(col < 16, value - high, 0.0)
    ahead_ref[...] = jnp.where(iota(shape, 0) < 48, high, low).astype(jnp.bfloat16)
    shape = (32, LANES)
    row, col = iota(shape, 0), iota(shape, 1)
    comp = row & 15
    speed = speeds_at(comp)
    times = jnp.broadcast_to(row_times[0:1], shape)
    basis = rotated_cosine(times * speed, comp & 1)
    other = col & 15
    turn = jnp.where(other == (comp ^ 1), jnp.where((comp & 1) == 0, -speed, speed), 0.0)
    value = jnp.where(col < 32, turn, basis)
    high = high_part(value)
    low_used = (col < 16) | ((col >= 32) & (col < 80))
    low = jnp.where(low_used, value - high, 0.0)
    back_ref[...] = jnp.where(row < 16, high, low).astype(jnp.bfloat16)


def kernel(
    tide_hbm, forcing_hbm, wet_hbm, band_hbm, drag_ref, stiff_ref, times_ref, zonal_hbm, meridional_hbm,
    out_ref,
    tide, forcing, wet_int, band, zonal_raw, mer_raw,
    wet, drag, stiff, ahead, back, zonal_w, mer_high, mer_low,
    cur, mix, back_terms, terms, halo_out, halo_in, fix_out, fix_in, fix, end_out, end_in, mid_out, mid_in, mid, zonal_lhs,
    fwd_out, fwd_in, ret_out, ret_in,
    local_sem, halo_send, halo_recv, fix_send, fix_recv, end_send, end_recv, mid_send, mid_recv, fwd_send, fwd_recv, ret_send, ret_recv,
):
    samp = lax.axis_index("samp")
    space = lax.axis_index("space")
    n_samp = lax.axis_size("samp")
    n_space = lax.axis_size("space")
    rank = space % RANKS
    base = space - rank
    chip, core = rank // 2, rank % 2
    owned = rank // 2

    loads = [
        pltpu.make_async_copy(wet_hbm, wet_int, local_sem.at[0]),
        pltpu.make_async_copy(band_hbm, band, local_sem.at[1]),
        pltpu.make_async_copy(tide_hbm, tide, local_sem.at[2]),
        pltpu.make_async_copy(forcing_hbm, forcing, local_sem.at[3]),
        pltpu.make_async_copy(zonal_hbm.at[owned], zonal_raw, local_sem.at[4]),
        pltpu.make_async_copy(meridional_hbm.at[owned], mer_raw, local_sem.at[5]),
    ]
    for load in loads:
        load.start()

    north = {"space": (space + n_space - 1) % n_space}
    south = {"space": (space + 1) % n_space}
    west = {"samp": (samp + n_samp - 1) % n_samp}
    east = {"samp": (samp + 1) % n_samp}
    across = {"space": (space + RANKS) % n_space}

    peers = []
    for dy, dc in OFFSETS:
        peers.append(((chip + dy) % CHIPS) * 2 + (core + dc) % 2)

    barrier = pltpu.get_barrier_semaphore()
    for target in [north, south, west, east, across] + [{"space": base + peer} for peer in peers]:
        pl.semaphore_signal(barrier, inc=1, device_id=target, device_id_type=MESH)

    build_factors(times_ref, ahead, back)

    loads[0].wait()
    loads[1].wait()
    wet[...] = wet_int[...].astype(jnp.float32)
    drags = jnp.zeros((ROWS, LANES), jnp.float32)
    stiffs = jnp.zeros((ROWS, LANES), jnp.float32)
    for level in range(drag_ref.shape[0]):
        here = band[...] == level
        drags = jnp.where(here, drag_ref[level], drags)
        stiffs = jnp.where(here, stiff_ref[level], stiffs)
    drag[...] = drags * (2.0 / SAMPLES)
    stiff[...] = stiffs

    tile = (COMPS, LANES)
    lane = iota(tile, 1)
    block = (ROWS, LANES)
    block_row, block_lane = iota(block, 0), iota(block, 1)
    has_north = (space > 0).astype(jnp.float32)
    has_south = (space < n_space - 1).astype(jnp.float32)

    def shift(value, amount):
        amount = amount % LANES
        return value if amount == 0 else pltpu.roll(value, amount, 1)

    def comps(r):
        return pl.ds(r * COMPS, COMPS)

    def spread(ref, r):
        return jnp.broadcast_to(ref[pl.ds(r, 1), :], tile)

    def piece(rank_index, rows=ROWS):
        return pl.ds(pl.multiple_of(rank_index * rows, rows), rows)

    def columns_to_lanes(value, first_lane):
        picked = jnp.where(block_lane == block_row + first_lane, jnp.broadcast_to(value, block), 0.0)
        return picked

    def set_state(it, r, value):
        cur[it, comps(r), :] = value
        high, low = split(value)
        cols = pl.ds(r * LANES, LANES)
        mix[0:16, cols] = high
        mix[16:32, cols] = low

    def remote(source, target, send, recv, device):
        return pltpu.make_async_remote_copy(
            src_ref=source, dst_ref=target, send_sem=send, recv_sem=recv, device_id=device, device_id_type=MESH
        )

    def exchange(source, target, send, recv, rows):
        copies = []
        for peer in peers:
            copy = remote(
                source.at[piece(peer, rows), :], target.at[piece(rank, rows), :], send.at[peer], recv.at[rank],
                {"space": base + peer},
            )
            copy.start()
            copies.append(copy)
        target[piece(rank, rows), :] = source[piece(rank, rows), :]
        return copies

    def await_piece(peer, source, target, send, recv, rows):
        remote(
            source.at[piece(rank, rows), :], target.at[piece(peer, rows), :], send.at[peer], recv.at[peer],
            {"space": base + peer},
        ).wait_recv()

    def exchange_half(half, source, target, send, recv, spot):
        copies = []
        for peer in peers:
            copy = remote(
                source.at[spot(half, peer), :], target.at[place(half, rank), :], send.at[half, peer],
                recv.at[half, rank], {"space": base + peer},
            )
            copy.start()
            copies.append(copy)
        target[place(half, rank), :] = source[spot(half, rank), :]
        return copies

    def await_half(half, peer, source, target, send, recv, spot):
        remote(
            source.at[spot(half, rank), :], target.at[place(half, peer), :], send.at[half, peer],
            recv.at[half, peer], {"space": base + peer},
        ).wait_recv()

    def place(half, rank_index):
        return pl.ds(pl.multiple_of(rank_index * ROWS + half * HALF, HALF), HALF)

    def solved(half, rank_index):
        return pl.ds(pl.multiple_of(half * RANKS * HALF + rank_index * HALF, HALF), HALF)

    def solved_rows(half, owner):
        return pl.ds(half * RANKS * HALF + owner * HALF, HALF)

    def friction(low_row=0, high_row=ROWS):
        for start in range(low_row, high_row, 4):
            cols = pl.ds(start * LANES, 4 * LANES)
            both = jnp.dot(ahead[...], mix[0:32, cols], preferred_element_type=jnp.float32)
            velocity = both[:SAMPLES] + both[SAMPLES:]
            for q in range(4):
                r = start + q
                part = velocity[:, q * LANES:(q + 1) * LANES]
                stress = jnp.broadcast_to(drag[pl.ds(r, 1), :], part.shape) * jnp.abs(part) * part
                high, low = split(stress)
                mix[32:80, pl.ds(r * LANES, LANES)] = high
                mix[80:128, pl.ds(r * LANES, LANES)] = low
            both = jnp.dot(back[...], mix[:, cols], preferred_element_type=jnp.float32)
            back_terms[:, cols] = both[:COMPS] + both[COMPS:]

    def local_terms(it, low_row, high_row):
        for r in range(low_row, high_row):
            value = cur[it, comps(r), :]
            left = jnp.where(lane == 0, 0.0, shift(value, 1))
            right = jnp.where(lane == LANES - 1, 0.0, shift(value, LANES - 1))
            neighbours = left + right
            if r > 0:
                neighbours = neighbours + cur[it, comps(r - 1), :]
            if r < high_row - 1:
                neighbours = neighbours + cur[it, comps(r + 1), :]
            total = value + back_terms[:, pl.ds(r * LANES, LANES)] + spread(stiff, r) * (4.0 * value - neighbours)
            terms[comps(r), :] = total

    def local_residual(it, low_row, high_row):
        count = high_row - low_row
        for c in range(COMPS):
            rows = pl.ds(c * ROWS + low_row, count)
            fallen = terms[pl.ds(low_row * COMPS + c, count, stride=COMPS), :]
            fwd_out[it, rows, :] = wet[low_row:high_row] * (forcing[rows, :] - fallen)

    def edge_terms(owner, it):
        value = fwd_in[it, piece(owner), :]
        west_row = jnp.broadcast_to(fix[pl.ds(owner, 1), :], block)
        east_row = jnp.broadcast_to(fix[pl.ds(owner + RANKS, 1), :], block)
        north_row = jnp.broadcast_to(fix[pl.ds(owner + 2 * RANKS, 1), :], block)
        south_row = jnp.broadcast_to(fix[pl.ds(owner + 3 * RANKS, 1), :], block)
        same = block_lane == block_row
        west_col = jnp.sum(jnp.where(same, west_row, 0.0), axis=1, keepdims=True)
        east_col = jnp.sum(jnp.where(same, east_row, 0.0), axis=1, keepdims=True)
        value = value + jnp.where(block_lane == 0, west_col, 0.0) + jnp.where(block_lane == LANES - 1, east_col, 0.0)
        value = value + jnp.where(block_row == 0, north_row, 0.0) + jnp.where(block_row == ROWS - 1, south_row, 0.0)
        if it == 1:
            mid_row = jnp.broadcast_to(mid[pl.ds(owner, 1), :], block)
            value = value + jnp.where(block_row == HALF - 1, mid_row, 0.0)
        high, low = split(value)
        zonal_lhs[piece(owner), 0:LANES] = high
        zonal_lhs[piece(owner), LANES:2 * LANES] = low

    def solve(it):
        both = jnp.dot(zonal_lhs[...], zonal_w[...], preferred_element_type=jnp.float32)
        high, low = split(both[:, :LANES] + both[:, LANES:])
        pair = jnp.concatenate([high, low], axis=1)
        copies = []
        for half in range(2):
            rows = pl.ds(half * RANKS * HALF, RANKS * HALF)
            both = jnp.dot(mer_high[rows, :], pair, preferred_element_type=jnp.float32)
            third = jnp.dot(mer_low[rows, :], high, preferred_element_type=jnp.float32)
            ret_out[it, rows, :] = both[:, :LANES] + both[:, LANES:] + third
            copies.extend(exchange_half(half, *returns(it)))
        return copies

    def returns(it):
        return ret_out.at[it], ret_in.at[it], ret_send.at[it], ret_recv.at[it], solved

    pending = []
    loads[2].wait()
    first = jnp.zeros(tile, jnp.float32)
    last = jnp.zeros(tile, jnp.float32)
    for r in range(ROWS):
        value = spread(wet, r) * tide[pl.ds(r, COMPS, stride=ROWS), :]
        set_state(0, r, value)
        first = jnp.where(lane == r, shift(value, r), first)
        last = jnp.where(lane == r, shift(value, r + 1), last)
    wets = wet[...]
    strength = wets * stiff[...]
    packed = jnp.sum(
        columns_to_lanes(wets[:, 0:1], 0)
        + columns_to_lanes(wets[:, LANES - 1:LANES], 32)
        + columns_to_lanes(strength[:, 0:1], 64)
        + columns_to_lanes(strength[:, LANES - 1:LANES], 96),
        axis=0,
        keepdims=True,
    )
    for slot, value, extra in (
        (0, cur[0, comps(ROWS - 1), :], wets[ROWS - 1:ROWS]),
        (1, cur[0, comps(0), :], wets[0:1]),
        (2, last, shift(packed, LANES - 32)),
        (3, first, packed),
    ):
        halo_out[slot, 0:COMPS, :] = value
        halo_out[slot, COMPS:COMPS + 8, :] = jnp.broadcast_to(extra, (8, LANES))
    friction()
    pl.semaphore_wait(barrier, 5 + len(peers))
    halos = []
    for slot, device in ((2, east), (3, west), (0, south), (1, north)):
        copy = remote(halo_out.at[slot], halo_in.at[slot], halo_send.at[slot], halo_recv.at[slot], device)
        copy.start()
        halos.append(copy)
    pending.extend(halos)
    local_terms(0, 0, ROWS)
    loads[3].wait()
    local_residual(0, 0, ROWS)
    fwd = (fwd_out.at[0], fwd_in.at[0], fwd_send.at[0, 0], fwd_recv.at[0, 0], ROWS)
    pending.extend(exchange(*fwd))

    for copy in halos:
        copy.wait_recv()
    sides = (
        (2, shift(packed, 64)),
        (3, shift(packed, 32)),
        (0, strength[0:1] * has_north),
        (1, strength[ROWS - 1:ROWS] * has_south),
    )
    for j, (slot, factor) in enumerate(sides):
        factors = jnp.broadcast_to(factor, tile)
        near = jnp.broadcast_to(halo_in[slot, COMPS:COMPS + 1, :], tile)
        fix_out[pl.ds(j, COMPS, stride=8), :] = factors * halo_in[slot, 0:COMPS, :]
        fix_out[pl.ds(4 + j, COMPS, stride=8), :] = 0.25 * factors * near
    fixes = (fix_out, fix_in, fix_send, fix_recv, 8)
    pending.extend(exchange(*fixes))
    factors = jnp.broadcast_to(strength[HALF - 1:HALF], tile)
    mid_out[pl.ds(0, COMPS, stride=8), :] = factors * cur[0, comps(HALF), :]
    mid_out[pl.ds(1, COMPS, stride=8), :] = 0.25 * factors * jnp.broadcast_to(wets[HALF:HALF + 1], tile)
    for j in range(2, 8):
        mid_out[pl.ds(j, COMPS, stride=8), :] = jnp.zeros(tile, jnp.float32)
    mids = (mid_out, mid_in, mid_send, mid_recv, 8)
    pending.extend(exchange(*mids))

    loads[4].wait()
    loads[5].wait()
    high, low = split(jnp.transpose(zonal_raw[...]))
    zonal_w[0:128, 0:128] = high
    zonal_w[0:128, 128:256] = low
    zonal_w[128:256, 0:128] = high
    zonal_w[128:256, 128:256] = jnp.zeros((LANES, LANES), jnp.bfloat16)
    for owner in range(RANKS):
        for half in range(2):
            start = owner * ROWS + half * HALF
            high, low = split(mer_raw[start:start + HALF, :])
            mer_high[solved_rows(half, owner), :] = high
            mer_low[solved_rows(half, owner), :] = low

    for peer in peers:
        await_piece(peer, *fwd)
    for peer in peers:
        await_piece(peer, *fixes)
    for j in range(4):
        fix[j * RANKS:(j + 1) * RANKS, :] = fix_in[pl.ds(j, RANKS, stride=8), :]
    for owner in range(RANKS):
        edge_terms(owner, 0)
    pending.extend(solve(0))

    for owner in range(RANKS):
        value = jnp.concatenate([ret_out[0, solved_rows(0, owner), :], ret_out[0, solved_rows(1, owner), :]], axis=0)
        end_out[owner:owner + 1, :] = jnp.sum(
            columns_to_lanes(value[:, 0:1], 0) + columns_to_lanes(value[:, LANES - 1:LANES], 32), axis=0, keepdims=True
        )
    end_out[16:17, :] = ret_out[0, 0:1, :]
    end_out[17:24, :] = jnp.broadcast_to(ret_out[0, LM - 1:LM, :], (7, LANES))
    ends = []
    for slot, device in ((0, east), (1, west), (2, across)):
        copy = remote(end_out, end_in.at[slot], end_send.at[slot], end_recv.at[slot], device)
        copy.start()
        ends.append(copy)
    pending.extend(ends)

    for half in range(2):
        for peer in peers:
            await_half(half, peer, *returns(0))
        low_row, high_row = half * HALF, (half + 1) * HALF
        for r in range(low_row, high_row):
            step = ret_in[0, pl.ds(r, COMPS, stride=ROWS), :]
            set_state(1, r, cur[0, comps(r), :] + 0.25 * spread(wet, r) * step)
        friction(low_row, high_row)
        local_terms(1, low_row, high_row)
        local_residual(1, low_row, high_row)
        pending.extend(exchange_half(half, fwd_out.at[1], fwd_in.at[1], fwd_send.at[1], fwd_recv.at[1], place))

    for peer in peers:
        await_piece(peer, *mids)
    for copy in ends:
        copy.wait_recv()
    norths = jnp.concatenate([end_in[2, 17:18, :], ret_out[0, pl.ds(RANKS * HALF + HALF - 1, RANKS, stride=HALF), :][:RANKS - 1]], axis=0)
    souths = jnp.concatenate([ret_out[0, pl.ds(0, RANKS, stride=HALF), :][1:], end_in[2, 16:17, :]], axis=0)
    steps = (shift(end_in[0, 0:RANKS, :], LANES - 32), end_in[1, 0:RANKS, :], norths, souths)
    for j, step in enumerate(steps):
        fix[j * RANKS:(j + 1) * RANKS, :] = (
            fix_in[pl.ds(j, RANKS, stride=8), :] + fix_in[pl.ds(4 + j, RANKS, stride=8), :] * step
        )
    mid[...] = mid_in[pl.ds(0, RANKS, stride=8), :] + mid_in[pl.ds(1, RANKS, stride=8), :] * ret_out[
        0, pl.ds(RANKS * HALF, RANKS, stride=HALF), :
    ]
    edge_terms(rank, 1)
    for peer in peers[::-1]:
        for half in range(2):
            await_half(half, peer, fwd_out.at[1], fwd_in.at[1], fwd_send.at[1], fwd_recv.at[1], place)
        edge_terms(peer, 1)
    leaving = solve(1)
    for copy in pending:
        copy.wait_send()
    for half in range(2):
        if half == 1:
            for copy in leaving:
                copy.wait_send()
        for peer in peers:
            await_half(half, peer, *returns(1))
        for c in range(COMPS):
            rows = pl.ds(c * ROWS + half * HALF, HALF)
            state = cur[1, pl.ds(half * HALF * COMPS + c, HALF, stride=COMPS), :]
            out_ref[rows, :] = state + 0.25 * wet[half * HALF:(half + 1) * HALF] * ret_in[1, rows, :]


def body(
    tide_state,
    forcing,
    wet_mask,
    depth_band,
    drag_table,
    stiff_table,
    sample_times,
    zonal_inverse,
    meridional_inverse,
):
    flat = (COMPS * ROWS, LANES)
    f32, bf16 = jnp.float32, jnp.bfloat16
    dma = pltpu.SemaphoreType.DMA
    any_spec = pl.BlockSpec(memory_space=pltpu.HBM)
    smem = pl.BlockSpec(memory_space=pltpu.SMEM)
    result = pl.pallas_call(
        kernel,
        out_shape=pltpu.VMEM(flat, f32),
        in_specs=[any_spec] * 4 + [smem] * 3 + [any_spec] * 2,
        out_specs=pl.BlockSpec(memory_space=pltpu.VMEM),
        scratch_shapes=[
            pltpu.VMEM(flat, f32),
            pltpu.VMEM(flat, f32),
            pltpu.VMEM((ROWS, LANES), jnp.int32),
            pltpu.VMEM((ROWS, LANES), jnp.int32),
            pltpu.VMEM((LANES, LANES), f32),
            pltpu.VMEM((LM, LM), f32),
            pltpu.VMEM((ROWS, LANES), f32),
            pltpu.VMEM((ROWS, LANES), f32),
            pltpu.VMEM((ROWS, LANES), f32),
            pltpu.VMEM((96, 32), bf16),
            pltpu.VMEM((32, LANES), bf16),
            pltpu.VMEM((256, 256), bf16),
            pltpu.VMEM((LM, LM), bf16),
            pltpu.VMEM((LM, LM), bf16),
            pltpu.VMEM((ITERS,) + flat, f32),
            pltpu.VMEM((LANES, ROWS * LANES), bf16),
            pltpu.VMEM((COMPS, ROWS * LANES), f32),
            pltpu.VMEM(flat, f32),
            pltpu.VMEM((4, COMPS + 8, LANES), f32),
            pltpu.VMEM((4, COMPS + 8, LANES), f32),
            pltpu.VMEM((8 * RANKS, LANES), f32),
            pltpu.VMEM((8 * RANKS, LANES), f32),
            pltpu.VMEM((4 * RANKS, LANES), f32),
            pltpu.VMEM((RANKS + 8, LANES), f32),
            pltpu.VMEM((3, RANKS + 8, LANES), f32),
            pltpu.VMEM((8 * RANKS, LANES), f32),
            pltpu.VMEM((8 * RANKS, LANES), f32),
            pltpu.VMEM((RANKS, LANES), f32),
            pltpu.VMEM((LM, 2 * LANES), bf16),
            pltpu.VMEM((ITERS,) + flat, f32),
            pltpu.VMEM((ITERS,) + flat, f32),
            pltpu.VMEM((ITERS,) + flat, f32),
            pltpu.VMEM((ITERS,) + flat, f32),
            dma((6,)),
            dma((4,)),
            dma((4,)),
            dma((RANKS,)),
            dma((RANKS,)),
            dma((3,)),
            dma((3,)),
            dma((RANKS,)),
            dma((RANKS,)),
            dma((ITERS, 2, RANKS)),
            dma((ITERS, 2, RANKS)),
            dma((ITERS, 2, RANKS)),
            dma((ITERS, 2, RANKS)),
        ],
        compiler_params=pltpu.CompilerParams(
            collective_id=0, has_side_effects=True, vmem_limit_bytes=60 * 1024 * 1024
        ),
        cost_estimate=pl.CostEstimate(flops=600000000, bytes_accessed=2500000, transcendentals=0),
    )(
        tide_state.reshape(flat),
        forcing.reshape(flat),
        wet_mask,
        depth_band,
        drag_table,
        stiff_table,
        sample_times,
        zonal_inverse,
        meridional_inverse,
    )
    return result.reshape(tide_state.shape)


def solution(mesh):
    grid = P(None, None, "space", "samp")
    return jax.shard_map(
        body,
        mesh=mesh,
        in_specs=(grid, grid, P("space", "samp"), P("space", "samp"), P(), P(), P(), P(), P()),
        out_specs=grid,
        check_vma=False,
    )
```

```python
import functools

import jax
import jax.numpy as jnp
from jax import lax
from jax.experimental import pallas as pl
from jax.experimental.pallas import tpu as pltpu
from jax.sharding import PartitionSpec as P

MESH = pl.DeviceIdType.MESH
ITERS = 2
ROWS = 32
HALF = 16
LANES = 128
COMPS = 16
SAMPLES = 48
RANKS = 16
CHIPS = 8
LM = 512

TIDAL_FREQUENCIES = (
    0.505868,
    0.5235988,
    0.4963657,
    0.5250316,
    0.2625162,
    0.2433523,
    0.2610812,
    0.2338335,
)

OFFSETS = [(dy, dc) for dy in (4, 3, 5, 2, 6, 1, 7) for dc in (0, 1)] + [(0, 1)]


def rotated_cosine(phase, quarter):
    turns = jnp.floor(phase * 0.63661977236758134308 + 0.5)
    rest = phase - turns * 1.5703125
    rest = rest - turns * 4.837512969970703125e-4
    rest = rest - turns * 7.54978995489188216e-8
    quadrant = (turns.astype(jnp.int32) + quarter) & 3
    square = rest * rest
    cosine = 1.0 + square * (
        -0.5 + square * (4.166664568298827e-2 + square * (-1.388731625493765e-3 + square * 2.443315711809948e-5))
    )
    sine = rest + rest * square * (
        -1.6666654611e-1 + square * (8.3321608736e-3 + square * -1.9515295891e-4)
    )
    value = jnp.where((quadrant & 1) == 1, -sine, cosine)
    return jnp.where(quadrant >= 2, -value, value)


def speeds_at(component):
    constituent = component >> 1
    speeds = jnp.zeros(component.shape, jnp.float32)
    for index, speed in enumerate(TIDAL_FREQUENCIES):
        speeds = jnp.where(constituent == index, jnp.float32(speed), speeds)
    return speeds


def high_part(value):
    return value.astype(jnp.bfloat16).astype(jnp.float32)


def split(value):
    high = value.astype(jnp.bfloat16)
    low = (value - high.astype(jnp.float32)).astype(jnp.bfloat16)
    return high, low


def iota(shape, dim):
    return lax.broadcasted_iota(jnp.int32, shape, dim)


def build_factors(times_ref, ahead_ref, back_ref):
    lane = iota((8, LANES), 1)
    row_times = jnp.zeros((8, LANES), jnp.float32)
    ahead_times = jnp.zeros((8, LANES), jnp.float32)
    for t in range(SAMPLES):
        value = times_ref[t]
        row_times = jnp.where((lane == 32 + t) | (lane == 80 + t), value, row_times)
        ahead_times = jnp.where((lane == t) | (lane == 48 + t), value, ahead_times)
    column_times = jnp.transpose(jnp.broadcast_to(ahead_times[0:1], (LANES, LANES)))[:96, :32]
    shape = (96, 32)
    col = iota(shape, 1)
    comp = col & 15
    value = rotated_cosine(column_times * speeds_at(comp), comp & 1)
    high = high_part(value)
    low = jnp.where(col < 16, value - high, 0.0)
    ahead_ref[...] = jnp.where(iota(shape, 0) < 48, high, low).astype(jnp.bfloat16)
    shape = (32, LANES)
    row, col = iota(shape, 0), iota(shape, 1)
    comp = row & 15
    speed = speeds_at(comp)
    times = jnp.broadcast_to(row_times[0:1], shape)
    basis = rotated_cosine(times * speed, comp & 1)
    other = col & 15
    turn = jnp.where(other == (comp ^ 1), jnp.where((comp & 1) == 0, -speed, speed), 0.0)
    value = jnp.where(col < 32, turn, basis)
    high = high_part(value)
    low_used = (col < 16) | ((col >= 32) & (col < 80))
    low = jnp.where(low_used, value - high, 0.0)
    back_ref[...] = jnp.where(row < 16, high, low).astype(jnp.bfloat16)


def kernel(
    tide_hbm, forcing_hbm, wet_hbm, band_hbm, drag_ref, stiff_ref, times_ref, zonal_hbm, meridional_hbm,
    out_ref,
    tide, forcing, wet_int, band, zonal_raw, mer_raw,
    wet, drag, stiff, ahead, back, zonal_w, mer_high, mer_low,
    cur, mix, back_terms, terms, halo_out, halo_in, fix_out, fix_in, fix, end_out, end_in, mid_out, mid_in, mid, zonal_lhs,
    fwd_out, fwd_in, ret_out, ret_in,
    local_sem, halo_send, halo_recv, fix_send, fix_recv, end_send, end_recv, mid_send, mid_recv, fwd_send, fwd_recv, ret_send, ret_recv,
):
    samp = lax.axis_index("samp")
    space = lax.axis_index("space")
    n_samp = lax.axis_size("samp")
    n_space = lax.axis_size("space")
    rank = space % RANKS
    base = space - rank
    chip, core = rank // 2, rank % 2
    owned = rank // 2

    loads = [
        pltpu.make_async_copy(wet_hbm, wet_int, local_sem.at[0]),
        pltpu.make_async_copy(band_hbm, band, local_sem.at[1]),
        pltpu.make_async_copy(tide_hbm, tide, local_sem.at[2]),
        pltpu.make_async_copy(forcing_hbm, forcing, local_sem.at[3]),
        pltpu.make_async_copy(zonal_hbm.at[owned], zonal_raw, local_sem.at[4]),
        pltpu.make_async_copy(meridional_hbm.at[owned], mer_raw, local_sem.at[5]),
    ]
    for load in loads:
        load.start()

    north = {"space": (space + n_space - 1) % n_space}
    south = {"space": (space + 1) % n_space}
    west = {"samp": (samp + n_samp - 1) % n_samp}
    east = {"samp": (samp + 1) % n_samp}
    across = {"space": (space + RANKS) % n_space}

    peers = []
    for dy, dc in OFFSETS:
        peers.append(((chip + dy) % CHIPS) * 2 + (core + dc) % 2)

    barrier = pltpu.get_barrier_semaphore()
    for target in [north, south, west, east, across] + [{"space": base + peer} for peer in peers]:
        pl.semaphore_signal(barrier, inc=1, device_id=target, device_id_type=MESH)

    build_factors(times_ref, ahead, back)

    loads[0].wait()
    loads[1].wait()
    wet[...] = wet_int[...].astype(jnp.float32)
    drags = jnp.zeros((ROWS, LANES), jnp.float32)
    stiffs = jnp.zeros((ROWS, LANES), jnp.float32)
    for level in range(drag_ref.shape[0]):
        here = band[...] == level
        drags = jnp.where(here, drag_ref[level], drags)
        stiffs = jnp.where(here, stiff_ref[level], stiffs)
    drag[...] = drags * (2.0 / SAMPLES)
    stiff[...] = stiffs

    tile = (COMPS, LANES)
    lane = iota(tile, 1)
    block = (ROWS, LANES)
    block_row, block_lane = iota(block, 0), iota(block, 1)
    has_north = (space > 0).astype(jnp.float32)
    has_south = (space < n_space - 1).astype(jnp.float32)

    def shift(value, amount):
        amount = amount % LANES
        return value if amount == 0 else pltpu.roll(value, amount, 1)

    def comps(r):
        return pl.ds(r * COMPS, COMPS)

    def spread(ref, r):
        return jnp.broadcast_to(ref[pl.ds(r, 1), :], tile)

    def piece(rank_index, rows=ROWS):
        return pl.ds(pl.multiple_of(rank_index * rows, rows), rows)

    def columns_to_lanes(value, first_lane):
        picked = jnp.where(block_lane == block_row + first_lane, jnp.broadcast_to(value, block), 0.0)
        return picked

    def set_state(it, r, value):
        cur[it, comps(r), :] = value
        high, low = split(value)
        cols = pl.ds(r * LANES, LANES)
        mix[0:16, cols] = high
        mix[16:32, cols] = low

    def remote(source, target, send, recv, device):
        return pltpu.make_async_remote_copy(
            src_ref=source, dst_ref=target, send_sem=send, recv_sem=recv, device_id=device, device_id_type=MESH
        )

    def exchange(source, target, send, recv, rows):
        copies = []
        for peer in peers:
            copy = remote(
                source.at[piece(peer, rows), :], target.at[piece(rank, rows), :], send.at[peer], recv.at[rank],
                {"space": base + peer},
            )
            copy.start()
            copies.append(copy)
        target[piece(rank, rows), :] = source[piece(rank, rows), :]
        return copies

    def await_piece(peer, source, target, send, recv, rows):
        remote(
            source.at[piece(rank, rows), :], target.at[piece(peer, rows), :], send.at[peer], recv.at[peer],
            {"space": base + peer},
        ).wait_recv()

    def exchange_half(half, source, target, send, recv, spot):
        copies = []
        for peer in peers:
            copy = remote(
                source.at[spot(half, peer), :], target.at[place(half, rank), :], send.at[half, peer],
                recv.at[half, rank], {"space": base + peer},
            )
            copy.start()
            copies.append(copy)
        target[place(half, rank), :] = source[spot(half, rank), :]
        return copies

    def await_half(half, peer, source, target, send, recv, spot):
        remote(
            source.at[spot(half, rank), :], target.at[place(half, peer), :], send.at[half, peer],
            recv.at[half, peer], {"space": base + peer},
        ).wait_recv()

    def place(half, rank_index):
        return pl.ds(pl.multiple_of(rank_index * ROWS + half * HALF, HALF), HALF)

    def solved(half, rank_index):
        return pl.ds(pl.multiple_of(half * RANKS * HALF + rank_index * HALF, HALF), HALF)

    def solved_rows(half, owner):
        return pl.ds(half * RANKS * HALF + owner * HALF, HALF)

    def friction(low_row=0, high_row=ROWS):
        for start in range(low_row, high_row, 4):
            cols = pl.ds(start * LANES, 4 * LANES)
            both = jnp.dot(ahead[...], mix[0:32, cols], preferred_element_type=jnp.float32)
            velocity = both[:SAMPLES] + both[SAMPLES:]
            for q in range(4):
                r = start + q
                part = velocity[:, q * LANES:(q + 1) * LANES]
                stress = jnp.broadcast_to(drag[pl.ds(r, 1), :], part.shape) * jnp.abs(part) * part
                high, low = split(stress)
                mix[32:80, pl.ds(r * LANES, LANES)] = high
                mix[80:128, pl.ds(r * LANES, LANES)] = low
            both = jnp.dot(back[...], mix[:, cols], preferred_element_type=jnp.float32)
            back_terms[:, cols] = both[:COMPS] + both[COMPS:]

    def local_terms(it, low_row, high_row):
        for r in range(low_row, high_row):
            value = cur[it, comps(r), :]
            left = jnp.where(lane == 0, 0.0, shift(value, 1))
            right = jnp.where(lane == LANES - 1, 0.0, shift(value, LANES - 1))
            neighbours = left + right
            if r > 0:
                neighbours = neighbours + cur[it, comps(r - 1), :]
            if r < high_row - 1:
                neighbours = neighbours + cur[it, comps(r + 1), :]
            total = value + back_terms[:, pl.ds(r * LANES, LANES)] + spread(stiff, r) * (4.0 * value - neighbours)
            terms[comps(r), :] = total

    def local_residual(it, low_row, high_row):
        count = high_row - low_row
        for c in range(COMPS):
            rows = pl.ds(c * ROWS + low_row, count)
            fallen = terms[pl.ds(low_row * COMPS + c, count, stride=COMPS), :]
            fwd_out[it, rows, :] = wet[low_row:high_row] * (forcing[rows, :] - fallen)

    def edge_terms(owner, it):
        value = fwd_in[it, piece(owner), :]
        west_row = jnp.broadcast_to(fix[pl.ds(owner, 1), :], block)
        east_row = jnp.broadcast_to(fix[pl.ds(owner + RANKS, 1), :], block)
        north_row = jnp.broadcast_to(fix[pl.ds(owner + 2 * RANKS, 1), :], block)
        south_row = jnp.broadcast_to(fix[pl.ds(owner + 3 * RANKS, 1), :], block)
        same = block_lane == block_row
        west_col = jnp.sum(jnp.where(same, west_row, 0.0), axis=1, keepdims=True)
        east_col = jnp.sum(jnp.where(same, east_row, 0.0), axis=1, keepdims=True)
        value = value + jnp.where(block_lane == 0, west_col, 0.0) + jnp.where(block_lane == LANES - 1, east_col, 0.0)
        value = value + jnp.where(block_row == 0, north_row, 0.0) + jnp.where(block_row == ROWS - 1, south_row, 0.0)
        if it == 1:
            mid_row = jnp.broadcast_to(mid[pl.ds(owner, 1), :], block)
            value = value + jnp.where(block_row == HALF - 1, mid_row, 0.0)
        high, low = split(value)
        zonal_lhs[piece(owner), 0:LANES] = high
        zonal_lhs[piece(owner), LANES:2 * LANES] = low

    def solve(it):
        both = jnp.dot(zonal_lhs[...], zonal_w[...], preferred_element_type=jnp.float32)
        high, low = split(both[:, :LANES] + both[:, LANES:])
        pair = jnp.concatenate([high, low], axis=1)
        copies = []
        for half in range(2):
            rows = pl.ds(half * RANKS * HALF, RANKS * HALF)
            both = jnp.dot(mer_high[rows, :], pair, preferred_element_type=jnp.float32)
            third = jnp.dot(mer_low[rows, :], high, preferred_element_type=jnp.float32)
            ret_out[it, rows, :] = both[:, :LANES] + both[:, LANES:] + third
            copies.extend(exchange_half(half, *returns(it)))
        return copies

    def returns(it):
        return ret_out.at[it], ret_in.at[it], ret_send.at[it], ret_recv.at[it], solved

    pending = []
    loads[2].wait()
    first = jnp.zeros(tile, jnp.float32)
    last = jnp.zeros(tile, jnp.float32)
    for r in range(ROWS):
        value = spread(wet, r) * tide[pl.ds(r, COMPS, stride=ROWS), :]
        set_state(0, r, value)
        first = jnp.where(lane == r, shift(value, r), first)
        last = jnp.where(lane == r, shift(value, r + 1), last)
    wets = wet[...]
    strength = wets * stiff[...]
    packed = jnp.sum(
        columns_to_lanes(wets[:, 0:1], 0)
        + columns_to_lanes(wets[:, LANES - 1:LANES], 32)
        + columns_to_lanes(strength[:, 0:1], 64)
        + columns_to_lanes(strength[:, LANES - 1:LANES], 96),
        axis=0,
        keepdims=True,
    )
    for slot, value, extra in (
        (0, cur[0, comps(ROWS - 1), :], wets[ROWS - 1:ROWS]),
        (1, cur[0, comps(0), :], wets[0:1]),
        (2, last, shift(packed, LANES - 32)),
        (3, first, packed),
    ):
        halo_out[slot, 0:COMPS, :] = value
        halo_out[slot, COMPS:COMPS + 8, :] = jnp.broadcast_to(extra, (8, LANES))
    friction()
    pl.semaphore_wait(barrier, 5 + len(peers))
    halos = []
    for slot, device in ((0, south), (1, north), (2, east), (3, west)):
        copy = remote(halo_out.at[slot], halo_in.at[slot], halo_send.at[slot], halo_recv.at[slot], device)
        copy.start()
        halos.append(copy)
    pending.extend(halos)
    local_terms(0, 0, ROWS)
    loads[3].wait()
    local_residual(0, 0, ROWS)
    fwd = (fwd_out.at[0], fwd_in.at[0], fwd_send.at[0, 0], fwd_recv.at[0, 0], ROWS)
    pending.extend(exchange(*fwd))

    for copy in halos:
        copy.wait_recv()
    sides = (
        (2, shift(packed, 64)),
        (3, shift(packed, 32)),
        (0, strength[0:1] * has_north),
        (1, strength[ROWS - 1:ROWS] * has_south),
    )
    for j, (slot, factor) in enumerate(sides):
        factors = jnp.broadcast_to(factor, tile)
        near = jnp.broadcast_to(halo_in[slot, COMPS:COMPS + 1, :], tile)
        fix_out[pl.ds(j, COMPS, stride=8), :] = factors * halo_in[slot, 0:COMPS, :]
        fix_out[pl.ds(4 + j, COMPS, stride=8), :] = 0.25 * factors * near
    fixes = (fix_out, fix_in, fix_send, fix_recv, 8)
    pending.extend(exchange(*fixes))
    factors = jnp.broadcast_to(strength[HALF - 1:HALF], tile)
    mid_out[pl.ds(0, COMPS, stride=8), :] = factors * cur[0, comps(HALF), :]
    mid_out[pl.ds(1, COMPS, stride=8), :] = 0.25 * factors * jnp.broadcast_to(wets[HALF:HALF + 1], tile)
    for j in range(2, 8):
        mid_out[pl.ds(j, COMPS, stride=8), :] = jnp.zeros(tile, jnp.float32)
    mids = (mid_out, mid_in, mid_send, mid_recv, 8)

    loads[4].wait()
    loads[5].wait()
    high, low = split(jnp.transpose(zonal_raw[...]))
    zonal_w[0:128, 0:128] = high
    zonal_w[0:128, 128:256] = low
    zonal_w[128:256, 0:128] = high
    zonal_w[128:256, 128:256] = jnp.zeros((LANES, LANES), jnp.bfloat16)
    for owner in range(RANKS):
        for half in range(2):
            start = owner * ROWS + half * HALF
            high, low = split(mer_raw[start:start + HALF, :])
            mer_high[solved_rows(half, owner), :] = high
            mer_low[solved_rows(half, owner), :] = low

    for peer in peers:
        await_piece(peer, *fwd)
    for peer in peers:
        await_piece(peer, *fixes)
    for j in range(4):
        fix[j * RANKS:(j + 1) * RANKS, :] = fix_in[pl.ds(j, RANKS, stride=8), :]
    for owner in range(RANKS):
        edge_terms(owner, 0)
    pending.extend(solve(0))
    pending.extend(exchange(*mids))

    for owner in range(RANKS):
        value = jnp.concatenate([ret_out[0, solved_rows(0, owner), :], ret_out[0, solved_rows(1, owner), :]], axis=0)
        end_out[owner:owner + 1, :] = jnp.sum(
            columns_to_lanes(value[:, 0:1], 0) + columns_to_lanes(value[:, LANES - 1:LANES], 32), axis=0, keepdims=True
        )
    end_out[16:17, :] = ret_out[0, 0:1, :]
    end_out[17:24, :] = jnp.broadcast_to(ret_out[0, LM - 1:LM, :], (7, LANES))
    ends = []
    for slot, device in ((0, east), (1, west), (2, across)):
        copy = remote(end_out, end_in.at[slot], end_send.at[slot], end_recv.at[slot], device)
        copy.start()
        ends.append(copy)
    pending.extend(ends)

    for half in range(2):
        for peer in peers:
            await_half(half, peer, *returns(0))
        low_row, high_row = half * HALF, (half + 1) * HALF
        for r in range(low_row, high_row):
            step = ret_in[0, pl.ds(r, COMPS, stride=ROWS), :]
            set_state(1, r, cur[0, comps(r), :] + 0.25 * spread(wet, r) * step)
        friction(low_row, high_row)
        local_terms(1, low_row, high_row)
        local_residual(1, low_row, high_row)
        pending.extend(exchange_half(half, fwd_out.at[1], fwd_in.at[1], fwd_send.at[1], fwd_recv.at[1], place))

    for peer in peers:
        await_piece(peer, *mids)
    for copy in ends:
        copy.wait_recv()
    norths = jnp.concatenate([end_in[2, 17:18, :], ret_out[0, pl.ds(RANKS * HALF + HALF - 1, RANKS, stride=HALF), :][:RANKS - 1]], axis=0)
    souths = jnp.concatenate([ret_out[0, pl.ds(0, RANKS, stride=HALF), :][1:], end_in[2, 16:17, :]], axis=0)
    steps = (shift(end_in[0, 0:RANKS, :], LANES - 32), end_in[1, 0:RANKS, :], norths, souths)
    for j, step in enumerate(steps):
        fix[j * RANKS:(j + 1) * RANKS, :] = (
            fix_in[pl.ds(j, RANKS, stride=8), :] + fix_in[pl.ds(4 + j, RANKS, stride=8), :] * step
        )
    mid[...] = mid_in[pl.ds(0, RANKS, stride=8), :] + mid_in[pl.ds(1, RANKS, stride=8), :] * ret_out[
        0, pl.ds(RANKS * HALF, RANKS, stride=HALF), :
    ]
    edge_terms(rank, 1)
    for peer in peers[::-1]:
        for half in range(2):
            await_half(half, peer, fwd_out.at[1], fwd_in.at[1], fwd_send.at[1], fwd_recv.at[1], place)
        edge_terms(peer, 1)
    leaving = solve(1)
    for copy in pending:
        copy.wait_send()
    for half in range(2):
        if half == 1:
            for copy in leaving:
                copy.wait_send()
        for peer in peers:
            await_half(half, peer, *returns(1))
        for c in range(COMPS):
            rows = pl.ds(c * ROWS + half * HALF, HALF)
            state = cur[1, pl.ds(half * HALF * COMPS + c, HALF, stride=COMPS), :]
            out_ref[rows, :] = state + 0.25 * wet[half * HALF:(half + 1) * HALF] * ret_in[1, rows, :]


def body(
    tide_state,
    forcing,
    wet_mask,
    depth_band,
    drag_table,
    stiff_table,
    sample_times,
    zonal_inverse,
    meridional_inverse,
):
    flat = (COMPS * ROWS, LANES)
    f32, bf16 = jnp.float32, jnp.bfloat16
    dma = pltpu.SemaphoreType.DMA
    any_spec = pl.BlockSpec(memory_space=pltpu.HBM)
    smem = pl.BlockSpec(memory_space=pltpu.SMEM)
    result = pl.pallas_call(
        kernel,
        out_shape=pltpu.VMEM(flat, f32),
        in_specs=[any_spec] * 4 + [smem] * 3 + [any_spec] * 2,
        out_specs=pl.BlockSpec(memory_space=pltpu.VMEM),
        scratch_shapes=[
            pltpu.VMEM(flat, f32),
            pltpu.VMEM(flat, f32),
            pltpu.VMEM((ROWS, LANES), jnp.int32),
            pltpu.VMEM((ROWS, LANES), jnp.int32),
            pltpu.VMEM((LANES, LANES), f32),
            pltpu.VMEM((LM, LM), f32),
            pltpu.VMEM((ROWS, LANES), f32),
            pltpu.VMEM((ROWS, LANES), f32),
            pltpu.VMEM((ROWS, LANES), f32),
            pltpu.VMEM((96, 32), bf16),
            pltpu.VMEM((32, LANES), bf16),
            pltpu.VMEM((256, 256), bf16),
            pltpu.VMEM((LM, LM), bf16),
            pltpu.VMEM((LM, LM), bf16),
            pltpu.VMEM((ITERS,) + flat, f32),
            pltpu.VMEM((LANES, ROWS * LANES), bf16),
            pltpu.VMEM((COMPS, ROWS * LANES), f32),
            pltpu.VMEM(flat, f32),
            pltpu.VMEM((4, COMPS + 8, LANES), f32),
            pltpu.VMEM((4, COMPS + 8, LANES), f32),
            pltpu.VMEM((8 * RANKS, LANES), f32),
            pltpu.VMEM((8 * RANKS, LANES), f32),
            pltpu.VMEM((4 * RANKS, LANES), f32),
            pltpu.VMEM((RANKS + 8, LANES), f32),
            pltpu.VMEM((3, RANKS + 8, LANES), f32),
            pltpu.VMEM((8 * RANKS, LANES), f32),
            pltpu.VMEM((8 * RANKS, LANES), f32),
            pltpu.VMEM((RANKS, LANES), f32),
            pltpu.VMEM((LM, 2 * LANES), bf16),
            pltpu.VMEM((ITERS,) + flat, f32),
            pltpu.VMEM((ITERS,) + flat, f32),
            pltpu.VMEM((ITERS,) + flat, f32),
            pltpu.VMEM((ITERS,) + flat, f32),
            dma((6,)),
            dma((4,)),
            dma((4,)),
            dma((RANKS,)),
            dma((RANKS,)),
            dma((3,)),
            dma((3,)),
            dma((RANKS,)),
            dma((RANKS,)),
            dma((ITERS, 2, RANKS)),
            dma((ITERS, 2, RANKS)),
            dma((ITERS, 2, RANKS)),
            dma((ITERS, 2, RANKS)),
        ],
        compiler_params=pltpu.CompilerParams(
            collective_id=0, has_side_effects=True, vmem_limit_bytes=60 * 1024 * 1024
        ),
        cost_estimate=pl.CostEstimate(flops=600000000, bytes_accessed=2500000, transcendentals=0),
    )(
        tide_state.reshape(flat),
        forcing.reshape(flat),
        wet_mask,
        depth_band,
        drag_table,
        stiff_table,
        sample_times,
        zonal_inverse,
        meridional_inverse,
    )
    return result.reshape(tide_state.shape)


def solution(mesh):
    grid = P(None, None, "space", "samp")
    return jax.shard_map(
        body,
        mesh=mesh,
        in_specs=(grid, grid, P("space", "samp"), P("space", "samp"), P(), P(), P(), P(), P()),
        out_specs=grid,
        check_vma=False,
    )
```
